128 devices in a mesh: row: 8 (over y, z_hi), col: 16 (over z_lo, x, core).
Axes of the slice: x: 4, y: 4, z: 4 (z_hi: 2, z_lo: 2; z = z_hi * 2 + z_lo), core: 2. Of those that a mesh axis runs over, the one named last changes fastest.
Arguments:
- inputs: bfloat16 [768, 12288], P('row', 'col'), may hold values from -6 to 6
- out_grad: bfloat16 [768, 12288], P('row', 'col'), may hold values from -6 to 6
- gate_pre: bfloat16 [768, 24576], P('col', 'row'), may hold values from -8 to 8
- up_pre: bfloat16 [768, 24576], P('col', 'row'), may hold values from -6 to 6
- gate_weight: bfloat16 [12288, 24576], P('col', 'row'), may hold values from -0.0546875 to 0.0546875
- up_weight: bfloat16 [12288, 24576], P('col', 'row'), may hold values from -0.0546875 to 0.0546875
- down_weight: bfloat16 [24576, 12288], P('row', 'col'), may hold values from -0.0390625 to 0.0390625
Outputs:
- grad_input: bfloat16 [768, 12288], P('row', 'col')
- grad_gate: bfloat16 [12288, 24576], P('col', 'row')
- grad_up: bfloat16 [12288, 24576], P('col', 'row')
The draws below stay inside these ranges and needn't reach their ends.
All inputs are finite; a program needn't handle non-finite values.
Results may differ from the reference program's by a relative error of at most 0.0049.
Values may be sent and summed in bfloat16 or wider, within the bound.
A program may use at most 128 MiB of HBM per device.

```python
import jax
import jax.numpy as jnp
from jax import lax

D = 12288
FF = 24576
TOKENS = 768


def level_of(own_key, shape, pieces, low, high):
    gain = 1.0
    for dim, blocks in pieces:
        heights = jax.random.uniform(jax.random.fold_in(jax.random.fold_in(own_key, 6), dim), (blocks,), jnp.float32, low / len(pieces), high / len(pieces))
        gain = gain * jnp.repeat(jnp.exp(heights), shape[dim] // blocks).reshape((-1,) + (1,) * (len(shape) - 1 - dim))
    return gain


def noise(key, dims, spread, most, split=(), kind=jnp.bfloat16):
    level = level_of(key, dims, split, -0.22, 0.18) if split else 1.0
    array = jax.random.normal(key, dims, jnp.float32) * spread * level
    return jnp.minimum(jnp.maximum(array, -most), most).astype(kind)


def setup_inputs(seed: int = 0) -> dict:
    keys = jax.random.split(jax.random.key(seed), 8)
    return {
        "inputs": noise(keys[0], (TOKENS, D), 1.0, 6.0, ((0, 8), (1, 16))),
        "out_grad": noise(keys[1], (TOKENS, D), 0.5, 6.0, ((0, 8), (1, 16))),
        "gate_pre": noise(keys[2], (TOKENS, FF), 1.5, 8.0, ((0, 16), (1, 8))),
        "up_pre": noise(keys[3], (TOKENS, FF), 1.0, 6.0, ((0, 16), (1, 8))),
        "gate_weight": noise(keys[4], (D, FF), D ** -0.5, 0.0546875, ((0, 16), (1, 8))),
        "up_weight": noise(keys[5], (D, FF), D ** -0.5, 0.0546875, ((0, 16), (1, 8))),
        "down_weight": noise(keys[6], (FF, D), FF ** -0.5, 0.0390625, ((0, 8), (1, 16))),
    }


def swiglu_back(hidden_delta, gate_pre, up_pre):
    gate_vals = gate_pre.astype(jnp.float32)
    up_vals = up_pre.astype(jnp.float32)
    sigma = jax.nn.sigmoid(gate_vals)
    up_delta = (hidden_delta * gate_vals * sigma).astype(jnp.bfloat16)
    gate_delta = (hidden_delta * up_vals * sigma * (1.0 + gate_vals * (1.0 - sigma))).astype(jnp.bfloat16)
    return gate_delta, up_delta


def right_trans(left, right):
    return lax.dot_general(left, right, (((1,), (1,)), ((), ())), preferred_element_type=jnp.float32)


def left_trans(left, right):
    return lax.dot_general(left, right, (((0,), (0,)), ((), ())), preferred_element_type=jnp.float32)


def reference(inputs, out_grad, gate_pre, up_pre, gate_weight, up_weight, down_weight):
    hidden_delta = jnp.dot(out_grad, down_weight.T, preferred_element_type=jnp.float32)
    gate_delta, up_delta = swiglu_back(hidden_delta, gate_pre, up_pre)
    grad_input = (right_trans(gate_delta, gate_weight) + right_trans(up_delta, up_weight)).astype(jnp.bfloat16)
    grad_gate = left_trans(inputs, gate_delta).astype(jnp.bfloat16)
    grad_up = left_trans(inputs, up_delta).astype(jnp.bfloat16)
    return grad_input, grad_gate, grad_up
```

```python
import jax
import jax.numpy as jnp
from jax import lax
from jax.experimental import pallas as pl
from jax.experimental.pallas import tpu as pltpu
from jax.sharding import PartitionSpec as P

BF16 = jnp.bfloat16
F32 = jnp.float32
NY, NZH, NZL, NX, NK = 4, 2, 2, 4, 2
NP = NZL * NX
NJ = 3
NH = 2
TB = 16


def right_trans(left, right):
    return lax.dot_general(
        left, right, (((1,), (1,)), ((), ())), preferred_element_type=F32
    )


def left_trans(left, right):
    return lax.dot_general(
        left, right, (((0,), (0,)), ((), ())), preferred_element_type=F32
    )


def kernel(
    og_ref,
    in_ref,
    gp_ref,
    up_ref,
    gw_ref,
    uw_ref,
    dw_ref,
    gi_ref,
    dg_ref,
    du_ref,
    xg_ref,
    dwv,
    gwv,
    uwv,
    gpv,
    upv,
    og,
    xg,
    db,
    hs,
    hr,
    ho,
    zs,
    zr,
    xs,
    xr,
    gacc,
    gs,
    gr,
    gz,
    gzr,
    load_sem,
    s_og,
    r_og,
    s_in,
    r_in,
    s_rs,
    r_rs,
    s_ag,
    r_ag,
    s_gi,
    r_gi,
    out_sem,
):
    r = lax.axis_index("row")
    c = lax.axis_index("col")
    y, zh = r // 2, r % 2
    zl, x, k = c // 8, (c // 2) % 4, c % 2
    p = zl * NX + x
    pz = (1 - zl) * NX + x

    def xmod(d):
        return (x + d) % NX

    dev_k = (r, c + 1 - 2 * k)
    dev_zl = (r, (1 - zl) * 8 + x * 2 + k)
    dev_zh = (y * 2 + 1 - zh, c)

    def dev_x(d):
        return (r, zl * 8 + xmod(d) * 2 + k)

    def dev_y(d):
        return (((y + d) % NY) * 2 + zh, c)

    ff = dw_ref.shape[0]
    dl = dw_ref.shape[1]
    cw = ff // NH

    barrier = pltpu.get_barrier_semaphore()
    peers = [dev_k, dev_zl, dev_zh] + [dev_x(d) for d in (1, 2, 3)] + [dev_y(d) for d in (1, 2, 3)]
    for dev in peers:
        pl.semaphore_signal(barrier, 1, device_id=dev, device_id_type=pl.DeviceIdType.MESH)

    loads = {}

    def load(name, src, dst):
        cp = pltpu.make_async_copy(src, dst, load_sem.at[len(loads)])
        cp.start()
        loads[name] = cp

    load("og", og_ref, og.at[r])
    load("dw", dw_ref, dwv)
    load("in", in_ref, xg.at[r])
    load("gp", gp_ref, gpv)
    load("up", up_ref, upv)
    load("gw", gw_ref, gwv)
    load("uw", uw_ref, uwv)

    pl.semaphore_wait(barrier, len(peers))

    sent = []

    def send(src, dst, ssem, rsem, dev):
        cp = pltpu.make_async_remote_copy(
            src_ref=src,
            dst_ref=dst,
            send_sem=ssem,
            recv_sem=rsem,
            device_id=dev,
            device_id_type=pl.DeviceIdType.MESH,
        )
        cp.start()
        sent.append(cp)
        return cp

    ogc = {}
    for j in range(NJ):
        for n, dev in enumerate([dev_zh] + [dev_y(d) for d in (1, 2, 3)]):
            ogc[j, n] = send(og_ref.at[:, j], og.at[r, :, j], s_og.at[j, n], r_og.at[j, n], dev)
    rz = y * 2 + 1 - zh
    for j in range(NJ):
        ogc[j, 0].wait_recv()
        for n, d in enumerate((1, 2, 3)):
            ogc[j, 4 + n] = send(
                og.at[rz, :, j], og.at[rz, :, j], s_og.at[j, 4 + n], r_og.at[j, 4 + n], dev_y(d)
            )
    inc = {}
    inc[0] = send(in_ref, xg.at[r], s_in.at[0], r_in.at[0], dev_zh)

    rs = {}
    ag = {}
    gic = {}

    def cols(h):
        return pl.ds(h * cw, cw)

    def s0(j, h):
        if h == 0:
            for n in range(1, 7):
                ogc[j, n].wait_recv()
        u = j * NH + h
        left = jnp.concatenate(
            [og[:, 1 - k, j].reshape(NP * TB, dl), og[:, k, j].reshape(NP * TB, dl)], axis=0
        )
        nt = 512

        def tile(n, _):
            w = dwv[pl.ds(pl.multiple_of(h * cw + n * nt, nt), nt), :]
            out = right_trans(left, w)
            at = pl.ds(pl.multiple_of(n * nt, nt), nt)
            hs[u, :, :, at] = out[: NP * TB].astype(BF16).reshape(NP, TB, nt)
            ho[u, :, :, at] = out[NP * TB :].reshape(NP, TB, nt)
            return 0

        lax.fori_loop(0, cw // nt, tile, 0)
        rs[u, 0] = send(hs.at[u], hr.at[u], s_rs.at[u, 0], r_rs.at[u, 0], dev_k)

    def s1(j, h):
        u = j * NH + h
        rs[u, 0].wait_recv()

        def add(i, _):
            far = (1 - zl) * NX + i
            zs[u, i] = (ho[u, far] + hr[u, far].astype(F32)).astype(BF16)
            return 0

        lax.fori_loop(0, NX, add, 0)
        rs[u, 1] = send(zs.at[u], zr.at[u], s_rs.at[u, 1], r_rs.at[u, 1], dev_zl)

    def s2(j, h):
        u = j * NH + h
        rs[u, 1].wait_recv()
        for d in (1, 3, 2):
            q = xmod(d)
            near = zl * NX + q
            xs[u, d - 1] = (
                ho[u, near] + hr[u, near].astype(F32) + zr[u, q].astype(F32)
            ).astype(BF16)
            rs[u, 1 + d] = send(
                xs.at[u, d - 1], xr.at[u, d - 1], s_rs.at[u, 1 + d], r_rs.at[u, 1 + d], dev_x(d)
            )

    def piece(q, j, h):
        return db.at[:, q, k, j, :, cols(h)]

    def part(a, q, j, h):
        return db.at[a, q, k, j, :, cols(h)]

    def ag_send(u, n, ref, dev):
        ag[u, n] = send(ref, ref, s_ag.at[u, n], r_ag.at[u, n], dev)

    def s3(j, h):
        u = j * NH + h
        for d in (1, 3, 2):
            rs[u, 1 + d].wait_recv()
        hidden = ho[u, p] + hr[u, p].astype(F32) + zr[u, x].astype(F32)
        for d in (1, 2, 3):
            hidden = hidden + xr[u, d - 1].astype(F32)
        g = gpv[j, :, cols(h)].astype(F32)
        up = upv[j, :, cols(h)].astype(F32)
        s = jax.nn.sigmoid(g)
        db[1, p, k, j, :, cols(h)] = (hidden * g * s).astype(BF16)
        db[0, p, k, j, :, cols(h)] = (hidden * up * s * (1.0 + g * (1.0 - s))).astype(BF16)
        ref = piece(p, j, h)
        ag_send(u, 0, ref, dev_zl)
        ag_send(u, 1, ref, dev_x(1))
        ag_send(u, 2, ref, dev_x(3))
        ag_send(u, 3, ref, dev_k)

    def s4(j, h):
        u = j * NH + h
        ag[u, 0].wait_recv()
        ref = piece(pz, j, h)
        ag_send(u, 4, ref, dev_x(1))
        ag_send(u, 5, ref, dev_x(3))
        ag_send(u, 6, ref, dev_k)

    def relay(j, h, first, base, lane):
        u = j * NH + h
        lo = lane * NX + xmod(3)
        hi = lane * NX + xmod(1)
        ag[u, first].wait_recv()
        ag_send(u, base, part(0, lo, j, h), dev_x(1))
        ag_send(u, base + 1, piece(lo, j, h), dev_k)
        ag[u, first + 1].wait_recv()
        ag_send(u, base + 2, part(1, hi, j, h), dev_x(3))
        ag_send(u, base + 3, piece(hi, j, h), dev_k)

    def s5(j, h):
        relay(j, h, 1, 7, zl)

    def s6(j, h):
        relay(j, h, 4, 11, 1 - zl)

    def s7(j, h):
        u = j * NH + h
        ag[u, 7].wait_recv()
        ag[u, 9].wait_recv()
        ag_send(u, 15, piece(zl * NX + xmod(2), j, h), dev_k)

    def s8(j, h):
        u = j * NH + h
        ag[u, 11].wait_recv()
        ag[u, 13].wait_recv()
        ag_send(u, 16, piece((1 - zl) * NX + xmod(2), j, h), dev_k)

    outs = []

    def s9(j, h):
        u = j * NH + h
        for n in (3, 6, 8, 10, 12, 14, 15, 16):
            ag[u, n].wait_recv()
        for a, ref in ((0, dg_ref), (1, du_ref)):
            cp = pltpu.make_async_copy(
                db.at[a, :, :, j, :, cols(h)], ref.at[:, :, j, :, cols(h)], out_sem.at[u, a]
            )
            cp.start()
            outs.append(cp)
        nt = 256
        dgate = db[0, :, :, j, :, cols(h)].reshape(NP * NK * TB, cw)
        dup = db[1, :, :, j, :, cols(h)].reshape(NP * NK * TB, cw)

        def tile(n, _):
            rows = pl.ds(pl.multiple_of(n * nt, nt), nt)
            out = right_trans(dgate, gwv[rows, cols(h)]) + right_trans(dup, uwv[rows, cols(h)])
            if h > 0:
                out = out + gacc[j, :, rows]
            if h < NH - 1:
                gacc[j, :, rows] = out
            else:
                gacc[j, :, rows] = out
                gs[j, :, :, :, rows] = out.astype(BF16).reshape(NP, NK, TB, nt)
            return 0

        lax.fori_loop(0, dl // nt, tile, 0)
        if h == NH - 1:
            for d in (1, 3, 2):
                to = (y + d) % NY
                gic[j, d] = send(
                    gs.at[j, pl.ds(to * 2, 2)],
                    gr.at[j, d - 1],
                    s_gi.at[j, d],
                    r_gi.at[j, d],
                    dev_y(d),
                )

    def s10(j, h):
        for d in (1, 3, 2):
            gic[j, d].wait_recv()

        def total(q):
            own = gacc[j, pl.ds(pl.multiple_of((y * 2 + q) * NK * TB, NK * TB), NK * TB), :]
            acc = own.reshape(NK, TB, dl)
            for d in (1, 2, 3):
                acc = acc + gr[j, d - 1, q].astype(F32)
            return acc

        gz[j] = total(1 - zh).astype(BF16)
        gic[j, 0] = send(gz.at[j], gzr.at[j], s_gi.at[j, 0], r_gi.at[j, 0], dev_zh)
        own = total(zh)
        gacc[j, pl.ds(0, NK * TB), :] = own.reshape(NK * TB, dl)

    def s11(j, h):
        gic[j, 0].wait_recv()
        own = gacc[j, pl.ds(0, NK * TB), :].reshape(NK, TB, dl)
        gi_ref[:, j] = (own + gzr[j].astype(F32)).astype(BF16)

    def inputs_on():
        inc[0].wait_recv()
        loads["in"].wait()
        for n, d in enumerate((1, 2, 3)):
            ref = xg.at[pl.ds(y * 2, 2)]
            inc[1 + n] = send(ref, ref, s_in.at[1 + n], r_in.at[1 + n], dev_y(d))

    def inputs_done():
        for n in range(3):
            inc[1 + n].wait_recv()
        cp = pltpu.make_async_copy(xg, xg_ref, out_sem.at[NJ * NH, 0])
        cp.start()
        outs.append(cp)

    steps = [s0, s1, s2, s3, s4, s5, s6, s7, s8, s9]
    units = [(j, h) for j in range(NJ) for h in range(NH)]

    loads["og"].wait()
    loads["dw"].wait()
    lag = [0, 1, 2, 3, 4, 5, 6, 7, 8, 9]
    nu = len(units)
    done = set()
    for t in range(nu + lag[-1]):
        for n in reversed(range(len(steps))):
            i = t - lag[n]
            if 0 <= i < nu:
                if n == 3 and i == 0:
                    loads["gp"].wait()
                    loads["up"].wait()
                if n == 9 and i == 0:
                    loads["gw"].wait()
                    loads["uw"].wait()
                steps[n](*units[i])
        if t == 2:
            inputs_on()
        if t == 10:
            inputs_done()
        for j in range(NJ):
            last = lag[-1] + (j + 1) * NH - 1
            if t == last + 1 and t < nu + lag[-1]:
                s10(j, 0)
                done.add(j)
    for j in range(NJ):
        if j not in done:
            s10(j, 0)
    for j in range(NJ):
        s11(j, 0)
    for cp in outs:
        cp.wait()
    for cp in sent:
        cp.wait_send()


def exchange(out_grad, inputs, gate_pre, up_pre, gate_weight, up_weight, down_weight):
    ff, dl = down_weight.shape
    cw = ff // NH
    nu = NJ * NH
    tok = NP * NK * NJ * TB
    dma = pltpu.SemaphoreType.DMA
    vm = pltpu.VMEM
    hbm = pl.BlockSpec(memory_space=pl.ANY)
    outs = pl.pallas_call(
        kernel,
        out_shape=(
            jax.ShapeDtypeStruct((NK, NJ, TB, dl), BF16),
            jax.ShapeDtypeStruct((NP, NK, NJ, TB, ff), BF16),
            jax.ShapeDtypeStruct((NP, NK, NJ, TB, ff), BF16),
            jax.ShapeDtypeStruct((NP, NK, NJ, TB, dl), BF16),
        ),
        in_specs=[hbm] * 7,
        out_specs=(pl.BlockSpec(memory_space=pltpu.VMEM), hbm, hbm, hbm),
        scratch_shapes=[
            vm((ff, dl), BF16),
            vm((dl, ff), BF16),
            vm((dl, ff), BF16),
            vm((NJ, TB, ff), BF16),
            vm((NJ, TB, ff), BF16),
            vm((NP, NK, NJ, TB, dl), BF16),
            vm((NP, NK, NJ, TB, dl), BF16),
            vm((2, NP, NK, NJ, TB, ff), BF16),
            vm((nu, NP, TB, cw), BF16),
            vm((nu, NP, TB, cw), BF16),
            vm((nu, NP, TB, cw), F32),
            vm((nu, NX, TB, cw), BF16),
            vm((nu, NX, TB, cw), BF16),
            vm((nu, 3, TB, cw), BF16),
            vm((nu, 3, TB, cw), BF16),
            vm((NJ, NP * NK * TB, dl), F32),
            vm((NJ, NP, NK, TB, dl), BF16),
            vm((NJ, 3, 2, NK, TB, dl), BF16),
            vm((NJ, NK, TB, dl), BF16),
            vm((NJ, NK, TB, dl), BF16),
            dma((7,)),
            dma((NJ, 7)),
            dma((NJ, 7)),
            dma((4,)),
            dma((4,)),
            dma((nu, 5)),
            dma((nu, 5)),
            dma((nu, 17)),
            dma((nu, 17)),
            dma((NJ, 4)),
            dma((NJ, 4)),
            dma((nu + 1, 2)),
        ],
        compiler_params=pltpu.CompilerParams(
            collective_id=0, has_side_effects=True, vmem_limit_bytes=62 * 2**20
        ),
        cost_estimate=pl.CostEstimate(
            flops=6 * tok * dl * ff, bytes_accessed=16 * dl * ff, transcendentals=0
        ),
    )(
        out_grad.reshape(NK, NJ, TB, dl),
        inputs.reshape(NK, NJ, TB, dl),
        gate_pre.reshape(NJ, TB, ff),
        up_pre.reshape(NJ, TB, ff),
        gate_weight,
        up_weight,
        down_weight,
    )
    grad_input, gate_delta, up_delta, tokens = outs
    return (
        grad_input.reshape(NK * NJ * TB, dl),
        gate_delta.reshape(tok, ff),
        up_delta.reshape(tok, ff),
        tokens.reshape(tok, dl),
    )


def on_device(inputs, out_grad, gate_pre, up_pre, gate_weight, up_weight, down_weight):
    grad_input, gate_delta, up_delta, tokens = exchange(
        out_grad, inputs, gate_pre, up_pre, gate_weight, up_weight, down_weight
    )
    grad_gate = left_trans(tokens, gate_delta).astype(BF16)
    grad_up = left_trans(tokens, up_delta).astype(BF16)
    return (grad_input, grad_gate, grad_up)


def solution(mesh):
    placed = (
        P("row", "col"),
        P("row", "col"),
        P("col", "row"),
        P("col", "row"),
        P("col", "row"),
        P("col", "row"),
        P("row", "col"),
    )
    return jax.shard_map(
        on_device,
        mesh=mesh,
        in_specs=placed,
        out_specs=(P("row", "col"), P("col", "row"), P("col", "row")),
        check_vma=False,
    )
```

```python
import jax
import jax.numpy as jnp
from jax import lax
from jax.experimental import pallas as pl
from jax.experimental.pallas import tpu as pltpu
from jax.sharding import PartitionSpec as P

BF16 = jnp.bfloat16
F32 = jnp.float32
MESH = pl.DeviceIdType.MESH
NY, NZH, NZL, NX, NK = 4, 2, 2, 4, 2
NP = NZL * NX
NJ = 3
TB = 16

UNITS = ((0, 0, 1024), (0, 1024, 1024), (0, 2048, 1024), (1, 0, 1024), (1, 1024, 1024), (1, 2048, 1024), (2, 0, 1024), (2, 1024, 1024), (2, 2048, 1024))
BLOCKS = tuple(sorted({(c0, w) for _, c0, w in UNITS}))
WMAX = max(w for _, w in BLOCKS)

ORDER = (
    ("o0", 0), ("o1", 0), ("o0", 1), ("s0", 0), ("s0", 1), ("o1", 1), ("s0", 2), ("s1", 0),
    ("o0", 2), ("s1", 1), ("s1", 2), ("s0", 3), ("s0", 4), ("s0", 5), ("s1", 3), ("s2", 0),
    ("o1", 2), ("i0", 0), ("s2", 1), ("s3", 0), ("s1", 4), ("s2", 2), ("s0", 6), ("s0", 7),
    ("s3", 1), ("s1", 5), ("s0", 8), ("s2", 3), ("s5", 0), ("s3", 2), ("s1", 6), ("i1", 0),
    ("s5", 1), ("s4", 0), ("s3", 3), ("s7", 0), ("s1", 7), ("s5", 2), ("s2", 4), ("s7", 1),
    ("s4", 1), ("s6", 0), ("s5", 3), ("s7", 2), ("s2", 5), ("s4", 2), ("s3", 4), ("s1", 8),
    ("s6", 1), ("s8", 0), ("s7", 3), ("s2", 6), ("s9", 0), ("s4", 3), ("s3", 5), ("s6", 2),
    ("i2", 0), ("s5", 4), ("s2", 7), ("s8", 1), ("s4", 4), ("s9", 1), ("s3", 6), ("s6", 3),
    ("s2", 8), ("s5", 5), ("s8", 2), ("s4", 5), ("s7", 4), ("s9", 2), ("gs", 0), ("s4", 6),
    ("s3", 7), ("s6", 4), ("s5", 6), ("s8", 3), ("s9", 3), ("s3", 8), ("s7", 5), ("s4", 7),
    ("s6", 5), ("g10", 0), ("s6", 6), ("s4", 8), ("s5", 7), ("s8", 4), ("s7", 6), ("s9", 4),
    ("g11", 0), ("s5", 8), ("s6", 7), ("s8", 5), ("s8", 6), ("s9", 5), ("gs", 1), ("s6", 8),
    ("s9", 6), ("s7", 7), ("s7", 8), ("dw", 0), ("s8", 7), ("dw", 1), ("dw", 2), ("s8", 8),
    ("s9", 7), ("s9", 8), ("gs", 2), ("dw", 3), ("dw", 4), ("g10", 1), ("dw", 5), ("dw", 6),
    ("dw", 7), ("dw", 8), ("dw", 9), ("dw", 10), ("g11", 1), ("dw", 11), ("g11", 2),
)


def right_trans(left, right):
    return lax.dot_general(
        left, right, (((1,), (1,)), ((), ())), preferred_element_type=F32
    )


def kernel(
    og_ref,
    in_ref,
    gp_ref,
    up_ref,
    gw_ref,
    uw_ref,
    dw_ref,
    gi_ref,
    ga_ref,
    ua_ref,
    dwv,
    gwv,
    uwv,
    gpv,
    upv,
    og,
    xg,
    xt,
    db,
    hs,
    hr,
    ho,
    zs,
    zr,
    xs,
    xr,
    gacc,
    gs,
    gr,
    gz,
    gzr,
    load_sem,
    s_og,
    r_og,
    s_in,
    r_in,
    s_rs,
    r_rs,
    s_ag,
    r_ag,
    s_gi,
    r_gi,
):
    r = lax.axis_index("row")
    c = lax.axis_index("col")
    y, zh = r // 2, r % 2
    zl, x, k = c // 8, (c // 2) % 4, c % 2
    p = zl * NX + x
    pz = (1 - zl) * NX + x
    rz = y * 2 + 1 - zh

    def xmod(d):
        return (x + d) % NX

    def ymod(d):
        return (y + d) % NY

    dev_k = (r, c + 1 - 2 * k)
    dev_zl = (r, (1 - zl) * 8 + x * 2 + k)
    dev_zh = (rz, c)

    def dev_x(d):
        return (r, zl * 8 + xmod(d) * 2 + k)

    def dev_y(d, other=False):
        return (ymod(d) * 2 + (1 - zh if other else zh), c)

    dl = dw_ref.shape[1]

    barrier = pltpu.get_barrier_semaphore()
    peers = [dev_k, dev_zl, dev_zh]
    peers += [dev_x(d) for d in (1, 2, 3)]
    peers += [dev_y(d) for d in (1, 2, 3)] + [dev_y(d, True) for d in (1, 2, 3)]
    for dev in peers:
        pl.semaphore_signal(barrier, 1, device_id=dev, device_id_type=MESH)

    loads = {}

    def load(name, src, dst):
        cp = pltpu.make_async_copy(src, dst, load_sem.at[len(loads)])
        cp.start()
        loads[name] = cp

    load("og", og_ref, og.at[r])
    load("dw", dw_ref, dwv)
    load("in", in_ref, xg.at[r])
    load("gp", gp_ref, gpv)
    load("up", up_ref, upv)
    load("gw", gw_ref, gwv)
    load("uw", uw_ref, uwv)
    loaded = set()

    def need(*names):
        for name in names:
            if name not in loaded:
                loaded.add(name)
                loads[name].wait()

    pl.semaphore_wait(barrier, len(peers))

    sent = []
    got = {}

    def send(key, src, dst, ssem, rsem, dev):
        cp = pltpu.make_async_remote_copy(
            src_ref=src,
            dst_ref=dst,
            send_sem=ssem,
            recv_sem=rsem,
            device_id=dev,
            device_id_type=MESH,
        )
        cp.start()
        sent.append(cp)
        got[key] = cp

    def arrived(*keys):
        for key in keys:
            got.pop(key).wait_recv()

    def o0(j):
        src, dst = og_ref.at[:, j], og.at[r, :, j]
        targets = [dev_zh] + [dev_y(d) for d in (1, 3, 2)]
        if j == 0:
            targets += [dev_y(d, True) for d in (1, 3, 2)]
        for n, dev in enumerate(targets):
            send(("og", j, n), src, dst, s_og.at[j, n], r_og.at[j, n], dev)

    def o1(j):
        arrived(("og", j, 0))
        if j == 0:
            return
        ref = og.at[rz, :, j]
        for n, d in enumerate((1, 3, 2)):
            send(("og", j, 4 + n), ref, ref, s_og.at[j, 4 + n], r_og.at[j, 4 + n], dev_y(d))

    def i0(_):
        send(("in", 0), in_ref, xg.at[r], s_in.at[0], r_in.at[0], dev_zh)

    def i1(_):
        need("in")
        arrived(("in", 0))
        ref = xg.at[pl.ds(y * 2, 2)]
        for n, d in enumerate((1, 3, 2)):
            send(("in", 1 + n), ref, ref, s_in.at[1 + n], r_in.at[1 + n], dev_y(d))

    def i2(_):
        arrived(("in", 1), ("in", 2), ("in", 3))
        per = NK * NJ * TB

        def turn(n, _):
            cols = pl.ds(pl.multiple_of(n * 128, 128), 128)
            xt[cols, :] = xg[:, :, :, :, cols].reshape(NP * per, 128).T
            return 0

        lax.fori_loop(0, dl // 128, turn, 0)

    def cols_of(u):
        _, c0, w = UNITS[u]
        return pl.ds(c0, w)

    seen_og = set()

    def s0(u):
        j, c0, w = UNITS[u]
        need("og", "dw")
        if j not in seen_og:
            seen_og.add(j)
            arrived(*[("og", j, n) for n in range(1, 7)])
        left = jnp.concatenate(
            [og[:, 1 - k, j].reshape(NP * TB, dl), og[:, k, j].reshape(NP * TB, dl)], axis=0
        )
        nt = 512

        def tile(n, _):
            rows = pl.ds(pl.multiple_of(c0 + n * nt, nt), nt)
            out = right_trans(left, dwv[rows, :])
            at = pl.ds(pl.multiple_of(n * nt, nt), nt)
            hs[u, :, :, at] = out[: NP * TB].astype(BF16).reshape(NP, TB, nt)
            ho[u, :, :, at] = out[NP * TB :].reshape(NP, TB, nt)
            return 0

        lax.fori_loop(0, w // nt, tile, 0)
        send(("k", u), hs.at[u], hr.at[u], s_rs.at[u, 0], r_rs.at[u, 0], dev_k)

    def s1(u):
        arrived(("k", u))

        def add(i, _):
            far = (1 - zl) * NX + i
            zs[u, i] = (ho[u, far] + hr[u, far].astype(F32)).astype(BF16)
            return 0

        lax.fori_loop(0, NX, add, 0)
        send(("z", u), zs.at[u], zr.at[u], s_rs.at[u, 1], r_rs.at[u, 1], dev_zl)

    def s2(u):
        arrived(("z", u))
        for d in (1, 3, 2):
            q = xmod(d)
            near = zl * NX + q
            xs[u, d - 1] = (
                ho[u, near] + hr[u, near].astype(F32) + zr[u, q].astype(F32)
            ).astype(BF16)
            send(
                ("x", u, d),
                xs.at[u, d - 1],
                xr.at[u, d - 1],
                s_rs.at[u, 1 + d],
                r_rs.at[u, 1 + d],
                dev_x(d),
            )

    def piece(u, q):
        return db.at[:, q, k, UNITS[u][0], :, cols_of(u)]

    def part(u, a, q):
        return db.at[a, q, k, UNITS[u][0], :, cols_of(u)]

    def ag_send(u, n, ref, dev):
        send(("a", u, n), ref, ref, s_ag.at[u, n], r_ag.at[u, n], dev)

    def s3(u):
        need("gp", "up")
        arrived(("x", u, 1), ("x", u, 3), ("x", u, 2))
        j = UNITS[u][0]
        cols = cols_of(u)
        hidden = ho[u, p] + hr[u, p].astype(F32) + zr[u, x].astype(F32)
        for d in (1, 2, 3):
            hidden = hidden + xr[u, d - 1].astype(F32)
        g = gpv[j, :, cols].astype(F32)
        up = upv[j, :, cols].astype(F32)
        s = jax.nn.sigmoid(g)
        db[1, p, k, j, :, cols] = (hidden * g * s).astype(BF16)
        db[0, p, k, j, :, cols] = (hidden * up * s * (1.0 + g * (1.0 - s))).astype(BF16)
        ref = piece(u, p)
        ag_send(u, 0, ref, dev_zl)
        ag_send(u, 1, ref, dev_x(1))
        ag_send(u, 2, ref, dev_x(3))
        ag_send(u, 3, ref, dev_k)

    def s4(u):
        arrived(("a", u, 0))
        ref = piece(u, pz)
        ag_send(u, 4, ref, dev_x(1))
        ag_send(u, 5, ref, dev_x(3))
        ag_send(u, 6, ref, dev_k)

    def relay(u, first, base, lane):
        lo = lane * NX + xmod(3)
        hi = lane * NX + xmod(1)
        arrived(("a", u, first))
        ag_send(u, base, part(u, 0, lo), dev_x(1))
        arrived(("a", u, first + 1))
        ag_send(u, base + 1, part(u, 1, hi), dev_x(3))
        ag_send(u, base + 2, piece(u, lo), dev_k)
        ag_send(u, base + 3, piece(u, hi), dev_k)

    def s5(u):
        relay(u, 1, 7, zl)

    def s6(u):
        relay(u, 4, 11, 1 - zl)

    def s7(u):
        arrived(("a", u, 7), ("a", u, 8))
        ag_send(u, 15, piece(u, zl * NX + xmod(2)), dev_k)

    def s8(u):
        arrived(("a", u, 11), ("a", u, 12))
        ag_send(u, 16, piece(u, (1 - zl) * NX + xmod(2)), dev_k)

    begun = set()

    def s9(u):
        j, c0, w = UNITS[u]
        cols = cols_of(u)
        need("gw", "uw")
        arrived(*[("a", u, n) for n in (3, 6, 9, 10, 13, 14, 15, 16)])
        dgate = db[0, :, :, j, :, cols].reshape(NP * NK * TB, w)
        dup = db[1, :, :, j, :, cols].reshape(NP * NK * TB, w)
        out = right_trans(dgate, gwv[:, cols]) + right_trans(dup, uwv[:, cols])
        if j in begun:
            out = out + gacc[j]
        begun.add(j)
        gacc[j] = out

    def gs0(j):
        gs[j] = gacc[j].astype(BF16).reshape(NP, NK, TB, dl)
        for d in (1, 3, 2):
            q = ymod(d)
            if j < NJ - 1:
                send(
                    ("g", j, d),
                    gs.at[j, pl.ds(q * 2, 2)],
                    gr.at[j, d - 1],
                    s_gi.at[j, d],
                    r_gi.at[j, d],
                    dev_y(d),
                )
            else:
                for e in (0, 1):
                    dest = q * 2 + (zh if e == 0 else 1 - zh)
                    send(
                        ("g", j, d + 3 * e),
                        gs.at[j, dest],
                        gr.at[j, d - 1, e],
                        s_gi.at[j, d + 3 * e],
                        r_gi.at[j, d + 3 * e],
                        dev_y(d, e == 1),
                    )
        if j == NJ - 1:
            send(("g", j, 0), gs.at[j, rz], gzr.at[j], s_gi.at[j, 0], r_gi.at[j, 0], dev_zh)

    def rows_of(dest):
        return pl.ds(pl.multiple_of(dest * NK * TB, NK * TB), NK * TB)

    def g10(j):
        arrived(("g", j, 1), ("g", j, 3), ("g", j, 2))

        def total(q):
            acc = gacc[j, rows_of(y * 2 + q), :].reshape(NK, TB, dl)
            for d in (1, 2, 3):
                acc = acc + gr[j, d - 1, q].astype(F32)
            return acc

        gz[j] = total(1 - zh).astype(BF16)
        send(("g", j, 0), gz.at[j], gzr.at[j], s_gi.at[j, 0], r_gi.at[j, 0], dev_zh)
        own = total(zh).reshape(NK * TB, dl)
        gacc[j, rows_of(r), :] = own

    def g11(j):
        if j == NJ - 1:
            arrived(*[("g", j, n) for n in range(1, 7)])
        arrived(("g", j, 0))
        acc = gacc[j, rows_of(r), :].reshape(NK, TB, dl) + gzr[j].astype(F32)
        if j == NJ - 1:
            for d in (1, 2, 3):
                for e in (0, 1):
                    acc = acc + gr[j, d - 1, e].astype(F32)
        gi_ref[:, j] = acc.astype(BF16)

    def dw(n):
        c0, w = BLOCKS[n // 4]
        a, half = n % 4 // 2, n % 2
        cols = pl.ds(c0 + half * (w // 2), w // 2)
        right = db[a, :, :, :, :, cols].reshape(NP * NK * NJ * TB, w // 2)
        out = jnp.dot(xt[...], right, preferred_element_type=F32)
        (ga_ref, ua_ref)[a][:, cols] = out.astype(BF16)

    steps = dict(
        o0=o0, o1=o1, i0=i0, i1=i1, i2=i2, s0=s0, s1=s1, s2=s2, s3=s3, s4=s4, s5=s5, s6=s6,
        s7=s7, s8=s8, s9=s9, gs=gs0, g10=g10, g11=g11, dw=dw,
    )
    for name, arg in ORDER:
        steps[name](arg)
    for cp in sent:
        cp.wait_send()


def on_device(inputs, out_grad, gate_pre, up_pre, gate_weight, up_weight, down_weight):
    ff, dl = down_weight.shape
    nu = len(UNITS)
    tok = NP * NK * NJ * TB
    dma = pltpu.SemaphoreType.DMA
    vm = pltpu.VMEM
    hbm = pl.BlockSpec(memory_space=pl.ANY)
    whole = pl.BlockSpec(memory_space=pltpu.VMEM)
    grad_input, grad_gate, grad_up = pl.pallas_call(
        kernel,
        out_shape=(
            jax.ShapeDtypeStruct((NK, NJ, TB, dl), BF16),
            pltpu.VMEM((dl, ff), BF16),
            pltpu.VMEM((dl, ff), BF16),
        ),
        in_specs=[hbm] * 7,
        out_specs=(whole, whole, whole),
        scratch_shapes=[
            vm((ff, dl), BF16),
            vm((dl, ff), BF16),
            vm((dl, ff), BF16),
            vm((NJ, TB, ff), BF16),
            vm((NJ, TB, ff), BF16),
            vm((NP, NK, NJ, TB, dl), BF16),
            vm((NP, NK, NJ, TB, dl), BF16),
            vm((dl, tok), BF16),
            vm((2, NP, NK, NJ, TB, ff), BF16),
            vm((nu, NP, TB, WMAX), BF16),
            vm((nu, NP, TB, WMAX), BF16),
            vm((nu, NP, TB, WMAX), F32),
            vm((nu, NX, TB, WMAX), BF16),
            vm((nu, NX, TB, WMAX), BF16),
            vm((nu, 3, TB, WMAX), BF16),
            vm((nu, 3, TB, WMAX), BF16),
            vm((NJ, NP * NK * TB, dl), F32),
            vm((NJ, NP, NK, TB, dl), BF16),
            vm((NJ, 3, 2, NK, TB, dl), BF16),
            vm((NJ, NK, TB, dl), BF16),
            vm((NJ, NK, TB, dl), BF16),
            dma((7,)),
            dma((NJ, 7)),
            dma((NJ, 7)),
            dma((4,)),
            dma((4,)),
            dma((nu, 5)),
            dma((nu, 5)),
            dma((nu, 17)),
            dma((nu, 17)),
            dma((NJ, 7)),
            dma((NJ, 7)),
        ],
        compiler_params=pltpu.CompilerParams(
            collective_id=0, has_side_effects=True, vmem_limit_bytes=51 * 2**20
        ),
        cost_estimate=pl.CostEstimate(
            flops=10 * tok * dl * ff, bytes_accessed=10 * dl * ff, transcendentals=0
        ),
    )(
        out_grad.reshape(NK, NJ, TB, dl),
        inputs.reshape(NK, NJ, TB, dl),
        gate_pre.reshape(NJ, TB, ff),
        up_pre.reshape(NJ, TB, ff),
        gate_weight,
        up_weight,
        down_weight,
    )
    return (grad_input.reshape(NK * NJ * TB, dl), grad_gate, grad_up)


def solution(mesh):
    placed = (
        P("row", "col"),
        P("row", "col"),
        P("col", "row"),
        P("col", "row"),
        P("col", "row"),
        P("col", "row"),
        P("row", "col"),
    )
    return jax.shard_map(
        on_device,
        mesh=mesh,
        in_specs=placed,
        out_specs=(P("row", "col"), P("col", "row"), P("col", "row")),
        check_vma=False,
    )
```

```python
import jax
import jax.numpy as jnp
from jax import lax
from jax.experimental import pallas as pl
from jax.experimental.pallas import tpu as pltpu
from jax.sharding import PartitionSpec as P

BF16 = jnp.bfloat16
F32 = jnp.float32
MESH = pl.DeviceIdType.MESH
NY, NZH, NZL, NX, NK = 4, 2, 2, 4, 2
NP = NZL * NX
NJ = 3
TB = 16

UNITS = ((0, 2048, 1024), (0, 0, 1024), (0, 1024, 1024), (1, 0, 1024), (1, 2048, 1024), (1, 1024, 1024), (2, 0, 1024), (2, 1024, 1024), (2, 2048, 1024))
SUM_X_FIRST = (4, 3, 6, 2, 0)
GATHER_X_FIRST = (1, 0, 7, 5)
DIRECT_FIRST = False
BLOCKS = tuple(sorted({(c0, w) for _, c0, w in UNITS}))
WMAX = max(w for _, w in BLOCKS)

ORDER = (
    ("o0", 0), ("o1", 0), ("o0", 1), ("o1", 1), ("o0", 2), ("s0", 0), ("s0", 1), ("s0", 2),
    ("s1", 0), ("s1", 1), ("o1", 2), ("i0", 0), ("s1", 2), ("s0", 3), ("s0", 4), ("s0", 5),
    ("s1", 3), ("s1", 4), ("s1", 5), ("s2", 1), ("s2", 0), ("s0", 6), ("s0", 7), ("s0", 8),
    ("s1", 6), ("s2", 2), ("s1", 7), ("i1", 0), ("s1", 8), ("s2", 3), ("s2", 5), ("s3", 0),
    ("s3", 2), ("s2", 4), ("s3", 1), ("s2", 7), ("s2", 6), ("s2", 8), ("s3", 3), ("s3", 5),
    ("s5", 0), ("s4", 0), ("s5", 2), ("s4", 2), ("s3", 4), ("s5", 1), ("s4", 1), ("s3", 6),
    ("i2", 0), ("s3", 7), ("s4", 3), ("s3", 8), ("s5", 3), ("s4", 5), ("s5", 5), ("s7", 0),
    ("s7", 2), ("s6", 0), ("s6", 2), ("s4", 4), ("s5", 4), ("s7", 1), ("s6", 1), ("s5", 6),
    ("s4", 6), ("s5", 7), ("s4", 7), ("s6", 3), ("s4", 8), ("s5", 8), ("s7", 3), ("s7", 5),
    ("s8", 2), ("s6", 5), ("s9", 2), ("s6", 4), ("s7", 4), ("s8", 0), ("s7", 6), ("s8", 1),
    ("s9", 0), ("s6", 6), ("s9", 1), ("gs", 0), ("s6", 7), ("s7", 7), ("s8", 3), ("s6", 8),
    ("s8", 5), ("s9", 3), ("s7", 8), ("s8", 4), ("s9", 5), ("s8", 6), ("s9", 4), ("gs", 1),
    ("s8", 7), ("s8", 8), ("s9", 6), ("s9", 7), ("s9", 8), ("gs", 2), ("g10", 0), ("dw", 0),
    ("dw", 1), ("dw", 2), ("g10", 1), ("dw", 3), ("g11", 0), ("dw", 4), ("g11", 2), ("dw", 5),
    ("g11", 1),
)


def right_trans(left, right):
    return lax.dot_general(
        left, right, (((1,), (1,)), ((), ())), preferred_element_type=F32
    )


def kernel(
    og_ref,
    in_ref,
    gp_ref,
    up_ref,
    gw_ref,
    uw_ref,
    dw_ref,
    gi_ref,
    ga_ref,
    ua_ref,
    dwv,
    gwv,
    uwv,
    gpv,
    upv,
    og,
    xg,
    xt,
    db,
    hs,
    hr,
    ho,
    zs,
    zr,
    xs,
    xr,
    gacc,
    gs,
    gr,
    gz,
    gzr,
    load_sem,
    send_sem,
    r_og,
    r_in,
    r_rs,
    r_ag,
    r_gi,
):
    r = lax.axis_index("row")
    c = lax.axis_index("col")
    y, zh = r // 2, r % 2
    zl, x, k = c // 8, (c // 2) % 4, c % 2
    p = zl * NX + x
    pz = (1 - zl) * NX + x
    rz = y * 2 + 1 - zh

    def xmod(d):
        return (x + d) % NX

    def ymod(d):
        return (y + d) % NY

    dev_k = (r, c + 1 - 2 * k)
    dev_zl = (r, (1 - zl) * 8 + x * 2 + k)
    dev_zh = (rz, c)

    def dev_x(d):
        return (r, zl * 8 + xmod(d) * 2 + k)

    def dev_y(d, other=False):
        return (ymod(d) * 2 + (1 - zh if other else zh), c)

    dl = dw_ref.shape[1]

    barrier = pltpu.get_barrier_semaphore()
    peers = [dev_k, dev_zl, dev_zh]
    peers += [dev_x(d) for d in (1, 2, 3)]
    peers += [dev_y(d) for d in (1, 2, 3)]
    if DIRECT_FIRST:
        peers += [dev_y(d, True) for d in (1, 2, 3)]
    for dev in peers:
        pl.semaphore_signal(barrier, 1, device_id=dev, device_id_type=MESH)

    loads = {}

    def load(name, src, dst):
        cp = pltpu.make_async_copy(src, dst, load_sem.at[len(loads)])
        cp.start()
        loads[name] = cp

    load("og", og_ref, og.at[r])
    load("dw", dw_ref, dwv)
    load("in", in_ref, xg.at[r])
    load("gp", gp_ref, gpv)
    load("up", up_ref, upv)
    load("gw", gw_ref, gwv)
    load("uw", uw_ref, uwv)
    loaded = set()

    def need(*names):
        for name in names:
            if name not in loaded:
                loaded.add(name)
                loads[name].wait()

    pl.semaphore_wait(barrier, len(peers))

    def send(src, dst, ssem, rsem, dev):
        pltpu.make_async_remote_copy(
            src_ref=src,
            dst_ref=dst,
            send_sem=send_sem.at[ssem],
            recv_sem=rsem,
            device_id=dev,
            device_id_type=MESH,
        ).start()

    def arrived(ref, sem):
        pltpu.make_async_copy(ref, ref, sem).wait()

    def o0(j):
        src, dst = og_ref.at[:, j], og.at[r, :, j]
        send(src, dst, 0, r_og.at[j, 0], dev_zh)
        for d in (1, 3, 2):
            send(src, dst, 0, r_og.at[j, 1], dev_y(d))
        if j == 0 and DIRECT_FIRST:
            for d in (1, 3, 2):
                send(src, dst, 0, r_og.at[j, 1], dev_y(d, True))

    def o1(j):
        arrived(og.at[0, :, j], r_og.at[j, 0])
        if j > 0 or not DIRECT_FIRST:
            ref = og.at[rz, :, j]
            for d in (1, 3, 2):
                send(ref, ref, 0, r_og.at[j, 1], dev_y(d))

    def i0(_):
        send(in_ref, xg.at[r], 1, r_in.at[0], dev_zh)

    def i1(_):
        need("in")
        arrived(xg.at[0], r_in.at[0])
        ref = xg.at[pl.ds(y * 2, 2)]
        for d in (1, 3, 2):
            send(ref, ref, 1, r_in.at[1], dev_y(d))

    def i2(_):
        arrived(xg.at[pl.ds(0, 6)], r_in.at[1])
        per = NK * NJ * TB

        def turn(n, _):
            cols = pl.ds(pl.multiple_of(n * 128, 128), 128)
            xt[cols, :] = xg[:, :, :, :, cols].reshape(NP * per, 128).T
            return 0

        lax.fori_loop(0, dl // 128, turn, 0)

    def cols_of(u):
        _, c0, w = UNITS[u]
        return pl.ds(c0, w)

    seen_og = set()

    def s0(u):
        j, c0, w = UNITS[u]
        need("og", "dw")
        if j not in seen_og:
            seen_og.add(j)
            arrived(og.at[pl.ds(0, 6), :, j], r_og.at[j, 1])
        left = jnp.concatenate(
            [og[:, 1 - k, j].reshape(NP * TB, dl), og[:, k, j].reshape(NP * TB, dl)], axis=0
        )
        nt = 768 if w % 768 == 0 else 512

        def tile(n, _):
            rows = pl.ds(pl.multiple_of(c0 + n * nt, nt), nt)
            out = right_trans(left, dwv[rows, :])
            at = pl.ds(pl.multiple_of(n * nt, nt), nt)
            hs[u, :, :, at] = out[: NP * TB].astype(BF16).reshape(NP, TB, nt)
            ho[u, :, :, at] = out[NP * TB :].reshape(NP, TB, nt)
            return 0

        lax.fori_loop(0, w // nt, tile, 0)
        send(hs.at[u], hr.at[u], 3 + j, r_rs.at[u, 0], dev_k)

    def core_sum(u, q):
        return ho[u, q] + hr[u, q].astype(F32)

    def s1(u):
        j = UNITS[u][0]
        arrived(hr.at[u], r_rs.at[u, 0])
        if u in SUM_X_FIRST:
            for d in (1, 3, 2):
                for lane in range(NZL):
                    xs[u, d - 1, lane] = core_sum(u, lane * NX + xmod(d)).astype(BF16)
                send(xs.at[u, d - 1], xr.at[u, d - 1], 3 + j, r_rs.at[u, 1], dev_x(d))
        else:

            def add(i, _):
                zs[u, i] = core_sum(u, (1 - zl) * NX + i).astype(BF16)
                return 0

            lax.fori_loop(0, NX, add, 0)
            send(zs.at[u], zr.at[u], 3 + j, r_rs.at[u, 1], dev_zl)

    def s2(u):
        j = UNITS[u][0]
        if u in SUM_X_FIRST:
            arrived(xr.at[u], r_rs.at[u, 1])
            total = core_sum(u, pz)
            for d in (1, 2, 3):
                total = total + xr[u, d - 1, 1 - zl].astype(F32)
            zs[u, 0] = total.astype(BF16)
            send(zs.at[u, 0], zr.at[u, 0], 3 + j, r_rs.at[u, 2], dev_zl)
        else:
            arrived(zr.at[u], r_rs.at[u, 1])
            for d in (1, 3, 2):
                q = xmod(d)
                xs[u, d - 1, 0] = (core_sum(u, zl * NX + q) + zr[u, q].astype(F32)).astype(BF16)
                send(xs.at[u, d - 1, 0], xr.at[u, d - 1, 0], 3 + j, r_rs.at[u, 2], dev_x(d))

    def piece(u, q):
        return db.at[:, q, k, UNITS[u][0], :, cols_of(u)]

    def pieces(u, n):
        return db.at[:, pl.ds(0, n), 0, UNITS[u][0], :, cols_of(u)]

    def part(u, a, q):
        return db.at[a, q, k, UNITS[u][0], :, cols_of(u)]

    def ag_send(u, n, ref, dev):
        send(ref, ref, 3 + NJ + UNITS[u][0], r_ag.at[u, n], dev)

    def s3(u):
        need("gp", "up")
        j = UNITS[u][0]
        cols = cols_of(u)
        if u in SUM_X_FIRST:
            arrived(zr.at[u, 0], r_rs.at[u, 2])
            hidden = core_sum(u, p) + zr[u, 0].astype(F32)
            lane = zl
        else:
            arrived(xr.at[u, :, 0], r_rs.at[u, 2])
            hidden = core_sum(u, p) + zr[u, x].astype(F32)
            lane = 0
        for d in (1, 2, 3):
            hidden = hidden + xr[u, d - 1, lane].astype(F32)
        g = gpv[j, :, cols].astype(F32)
        up = upv[j, :, cols].astype(F32)
        s = jax.nn.sigmoid(g)
        db[1, p, k, j, :, cols] = (hidden * g * s).astype(BF16)
        db[0, p, k, j, :, cols] = (hidden * up * s * (1.0 + g * (1.0 - s))).astype(BF16)
        ref = piece(u, p)
        ag_send(u, 1, ref, dev_x(1))
        ag_send(u, 1, ref, dev_x(3))
        ag_send(u, 0, ref, dev_zl)
        ag_send(u, 5, ref, dev_k)

    def s4(u):
        arrived(pieces(u, 1), r_ag.at[u, 0])
        ref = piece(u, pz)
        if u not in GATHER_X_FIRST:
            ag_send(u, 2, ref, dev_x(1))
            ag_send(u, 2, ref, dev_x(3))
        ag_send(u, 5, ref, dev_k)

    def sides(u, first, then, lane, relay):
        lo = lane * NX + xmod(3)
        hi = lane * NX + xmod(1)
        arrived(pieces(u, 2), r_ag.at[u, first])
        if relay:
            ag_send(u, then, part(u, 0, lo), dev_x(1))
            ag_send(u, then, part(u, 1, hi), dev_x(3))
        if relay and u in GATHER_X_FIRST:
            ag_send(u, 2, piece(u, lo), dev_zl)
            ag_send(u, 2, piece(u, hi), dev_zl)
        ag_send(u, 5, piece(u, lo), dev_k)
        ag_send(u, 5, piece(u, hi), dev_k)

    def s5(u):
        sides(u, 1, 3, zl, True)

    def s6(u):
        sides(u, 2, 4, 1 - zl, u not in GATHER_X_FIRST)

    def s7(u):
        arrived(pieces(u, 1), r_ag.at[u, 3])
        ref = piece(u, zl * NX + xmod(2))
        if u in GATHER_X_FIRST:
            ag_send(u, 4, ref, dev_zl)
        ag_send(u, 5, ref, dev_k)

    def s8(u):
        arrived(pieces(u, 1), r_ag.at[u, 4])
        ag_send(u, 5, piece(u, (1 - zl) * NX + xmod(2)), dev_k)

    begun = set()

    def s9(u):
        j, c0, w = UNITS[u]
        cols = cols_of(u)
        need("gw", "uw")
        arrived(pieces(u, NP), r_ag.at[u, 5])
        dgate = db[0, :, :, j, :, cols].reshape(NP * NK * TB, w)
        dup = db[1, :, :, j, :, cols].reshape(NP * NK * TB, w)
        out = right_trans(dgate, gwv[:, cols]) + right_trans(dup, uwv[:, cols])
        if j in begun:
            out = out + gacc[j]
        begun.add(j)
        gacc[j] = out

    def gs0(j):
        gs[j] = gacc[j].astype(BF16).reshape(NP, NK, TB, dl)
        for d in (1, 3, 2):
            q = ymod(d) * 2
            if j < NJ - 1:
                send(gs.at[j, pl.ds(q, 2)], gr.at[j, d - 1], 2, r_gi.at[j, 1], dev_y(d))
            else:
                send(gs.at[j, q + zh], gr.at[j, d - 1, 0], 2, r_gi.at[j, 1], dev_y(d))
                send(gs.at[j, q + 1 - zh], gr.at[j, d - 1, 1], 2, r_gi.at[j, 1], dev_y(d, True))
        if j == NJ - 1:
            send(gs.at[j, rz], gzr.at[j], 2, r_gi.at[j, 0], dev_zh)

    def rows_of(dest):
        return pl.ds(pl.multiple_of(dest * NK * TB, NK * TB), NK * TB)

    def g10(j):
        arrived(gr.at[j], r_gi.at[j, 1])

        def total(q):
            acc = gacc[j, rows_of(y * 2 + q), :].reshape(NK, TB, dl)
            for d in (1, 2, 3):
                acc = acc + gr[j, d - 1, q].astype(F32)
            return acc

        gz[j] = total(1 - zh).astype(BF16)
        send(gz.at[j], gzr.at[j], 2, r_gi.at[j, 0], dev_zh)
        gacc[j, rows_of(r), :] = total(zh).reshape(NK * TB, dl)

    def g11(j):
        arrived(gzr.at[j], r_gi.at[j, 0])
        acc = gacc[j, rows_of(r), :].reshape(NK, TB, dl) + gzr[j].astype(F32)
        if j == NJ - 1:
            arrived(gr.at[j], r_gi.at[j, 1])
            for d in (1, 2, 3):
                for e in (0, 1):
                    acc = acc + gr[j, d - 1, e].astype(F32)
        gi_ref[:, j] = acc.astype(BF16)

    def dw(n):
        c0, w = BLOCKS[n // 2]
        cols = pl.ds(c0, w)
        right = db[n % 2, :, :, :, :, cols].reshape(NP * NK * NJ * TB, w)
        out = jnp.dot(xt[...], right, preferred_element_type=F32)
        (ga_ref, ua_ref)[n % 2][:, cols] = out.astype(BF16)

    steps = dict(
        o0=o0, o1=o1, i0=i0, i1=i1, i2=i2, s0=s0, s1=s1, s2=s2, s3=s3, s4=s4, s5=s5, s6=s6,
        s7=s7, s8=s8, s9=s9, gs=gs0, g10=g10, g11=g11, dw=dw,
    )
    for name, arg in ORDER:
        steps[name](arg)
    for n in range(3):
        arrived(og.at[pl.ds(0, 7)], send_sem.at[n])
    for j in range(NJ):
        arrived(db.at[0, pl.ds(0, 5), 0], send_sem.at[3 + j])
        arrived(db.at[:, pl.ds(0, 5), 0], send_sem.at[3 + NJ + j])


def store(gi, ga, ua, gi_out, ga_out, ua_out, sem):
    half = ga.shape[0] // 2
    top, low = pl.ds(0, half), pl.ds(half, half)
    copies = [(gi, gi_out)]
    for src, dst in ((ga, ga_out), (ua, ua_out)):
        copies += [(src.at[top], dst.at[top]), (src.at[low], dst.at[low])]
    started = []
    for n, (src, dst) in enumerate(copies):
        cp = pltpu.make_async_copy(src, dst, sem.at[n])
        cp.start()
        started.append(cp)
    for cp in started:
        cp.wait()


def on_device(inputs, out_grad, gate_pre, up_pre, gate_weight, up_weight, down_weight):
    ff, dl = down_weight.shape
    nu = len(UNITS)
    tok = NP * NK * NJ * TB
    dma = pltpu.SemaphoreType.DMA
    vm = pltpu.VMEM
    hbm = pl.BlockSpec(memory_space=pl.ANY)
    whole = pl.BlockSpec(memory_space=pltpu.VMEM)
    grad_input, grad_gate, grad_up = pl.pallas_call(
        kernel,
        out_shape=(
            pltpu.VMEM((NK, NJ, TB, dl), BF16),
            pltpu.VMEM((dl, ff), BF16),
            pltpu.VMEM((dl, ff), BF16),
        ),
        in_specs=[hbm] * 7,
        out_specs=(whole, whole, whole),
        scratch_shapes=[
            vm((ff, dl), BF16),
            vm((dl, ff), BF16),
            vm((dl, ff), BF16),
            vm((NJ, TB, ff), BF16),
            vm((NJ, TB, ff), BF16),
            vm((NP, NK, NJ, TB, dl), BF16),
            vm((NP, NK, NJ, TB, dl), BF16),
            vm((dl, tok), BF16),
            vm((2, NP, NK, NJ, TB, ff), BF16),
            vm((nu, NP, TB, WMAX), BF16),
            vm((nu, NP, TB, WMAX), BF16),
            vm((nu, NP, TB, WMAX), F32),
            vm((nu, NX, TB, WMAX), BF16),
            vm((nu, NX, TB, WMAX), BF16),
            vm((nu, 3, NZL, TB, WMAX), BF16),
            vm((nu, 3, NZL, TB, WMAX), BF16),
            vm((NJ, NP * NK * TB, dl), F32),
            vm((NJ, NP, NK, TB, dl), BF16),
            vm((NJ, 3, 2, NK, TB, dl), BF16),
            vm((NJ, NK, TB, dl), BF16),
            vm((NJ, NK, TB, dl), BF16),
            dma((7,)),
            dma((3 + 2 * NJ,)),
            dma((NJ, 2)),
            dma((2,)),
            dma((nu, 3)),
            dma((nu, 6)),
            dma((NJ, 2)),
        ],
        compiler_params=pltpu.CompilerParams(
            collective_id=0, has_side_effects=True, vmem_limit_bytes=48 * 2**20
        ),
        cost_estimate=pl.CostEstimate(
            flops=10 * tok * dl * ff, bytes_accessed=10 * dl * ff, transcendentals=0
        ),
    )(
        out_grad.reshape(NK, NJ, TB, dl),
        inputs.reshape(NK, NJ, TB, dl),
        gate_pre.reshape(NJ, TB, ff),
        up_pre.reshape(NJ, TB, ff),
        gate_weight,
        up_weight,
        down_weight,
    )
    grad_input, grad_gate, grad_up = pl.pallas_call(
        store,
        out_shape=(
            jax.ShapeDtypeStruct((NK, NJ, TB, dl), BF16),
            jax.ShapeDtypeStruct((dl, ff), BF16),
            jax.ShapeDtypeStruct((dl, ff), BF16),
        ),
        in_specs=[whole] * 3,
        out_specs=(hbm, hbm, hbm),
        scratch_shapes=[dma((5,))],
        compiler_params=pltpu.CompilerParams(vmem_limit_bytes=4 * 2**20),
    )(*(pltpu.with_memory_space_constraint(a, pltpu.VMEM) for a in (grad_input, grad_gate, grad_up)))
    return (grad_input.reshape(NK * NJ * TB, dl), grad_gate, grad_up)


def solution(mesh):
    placed = (
        P("row", "col"),
        P("row", "col"),
        P("col", "row"),
        P("col", "row"),
        P("col", "row"),
        P("col", "row"),
        P("row", "col"),
    )
    return jax.shard_map(
        on_device,
        mesh=mesh,
        in_specs=placed,
        out_specs=(P("row", "col"), P("col", "row"), P("col", "row")),
        check_vma=False,
    )
```

```python
import jax
import jax.numpy as jnp
from jax import lax
from jax.experimental import pallas as pl
from jax.experimental.pallas import tpu as pltpu
from jax.sharding import PartitionSpec as P

BF16 = jnp.bfloat16
F32 = jnp.float32
MESH = pl.DeviceIdType.MESH
NY, NZH, NZL, NX, NK = 4, 2, 2, 4, 2
NP = NZL * NX
NJ = 3
TB = 16

UNITS = ((0, 0, 768), (0, 2304, 768), (0, 1536, 768), (0, 768, 768), (1, 768, 768), (2, 0, 768), (1, 0, 768), (1, 1536, 768), (1, 2304, 768), (2, 2304, 768), (2, 1536, 768), (2, 768, 768))
SUM_X_FIRST = (6, 0)
GATHER_X_FIRST = (8, 11, 0, 4, 10)
AHEAD = (0, 3, 2, 1)
BLOCKS = tuple(sorted({(c0, w) for _, c0, w in UNITS}))
WMAX = max(w for _, w in BLOCKS)

ORDER = (
    ("o0", 0), ("p3", 0), ("p3", 1), ("p3", 2), ("p3", 3), ("p5", 0), ("o1", 0), ("o0", 1),
    ("p5", 1), ("o1", 1), ("o0", 2), ("p5", 2), ("o1", 2), ("p5", 3), ("p7", 0), ("p7", 1),
    ("s0", 0), ("p7", 2), ("s0", 1), ("p4", 0), ("p7", 3), ("s0", 2), ("s1", 0), ("p4", 1),
    ("s1", 1), ("s0", 3), ("s1", 2), ("p4", 2), ("i1", 0), ("p4", 3), ("s0", 4), ("s1", 3),
    ("s0", 6), ("s0", 7), ("s0", 8), ("p6", 0), ("s2", 1), ("s2", 0), ("s1", 4), ("p6", 1),
    ("s0", 5), ("s0", 9), ("s2", 2), ("s1", 6), ("s1", 5), ("s0", 10), ("p8", 0), ("s0", 11),
    ("s2", 3), ("s1", 7), ("p8", 1), ("s3", 0), ("s3", 1), ("p6", 2), ("p6", 3), ("s3", 2),
    ("s2", 4), ("s1", 8), ("s2", 6), ("s2", 5), ("s1", 10), ("s1", 9), ("s5", 0), ("s3", 3),
    ("s5", 1), ("p8", 2), ("s2", 7), ("p8", 3), ("s1", 11), ("s4", 0), ("s5", 2), ("s4", 1),
    ("s4", 2), ("s3", 4), ("s7", 0), ("i2", 0), ("s5", 3), ("s7", 1), ("s2", 8), ("s3", 5),
    ("s3", 6), ("s7", 2), ("s3", 7), ("s6", 1), ("s6", 2), ("s2", 10), ("s5", 4), ("s7", 3),
    ("s2", 9), ("s3", 8), ("s6", 0), ("s5", 5), ("s4", 3), ("s5", 6), ("s5", 7), ("s8", 1),
    ("s2", 11), ("s8", 2), ("s9", 1), ("s7", 4), ("s8", 0), ("s4", 4), ("s4", 5), ("s9", 2),
    ("s5", 8), ("s7", 5), ("s6", 3), ("s7", 6), ("s4", 6), ("s4", 7), ("s9", 0), ("s7", 7),
    ("s6", 4), ("s4", 8), ("s3", 10), ("s6", 5), ("s3", 9), ("s7", 8), ("s8", 3), ("s8", 4),
    ("s3", 11), ("s6", 6), ("s9", 3), ("s6", 7), ("s5", 10), ("s6", 8), ("s4", 10), ("s9", 4),
    ("s8", 5), ("s4", 9), ("gs", 0), ("s5", 9), ("s8", 8), ("s9", 5), ("s5", 11), ("s8", 6),
    ("s4", 11), ("s9", 8), ("s7", 10), ("s8", 7), ("s9", 6), ("dw", 0), ("s7", 9), ("s7", 11),
    ("s6", 9), ("s6", 10), ("s9", 7), ("gs", 1), ("s6", 11), ("dw", 1), ("s8", 10), ("g10", 0),
    ("s8", 9), ("s8", 11), ("s9", 10), ("s9", 9), ("s9", 11), ("gs", 2), ("dw", 4), ("g11", 0),
    ("dw", 5), ("g10", 1), ("dw", 6), ("dw", 7), ("dw", 2), ("dw", 3), ("g11", 1), ("g11", 2),
)


def right_trans(left, right):
    return lax.dot_general(
        left, right, (((1,), (1,)), ((), ())), preferred_element_type=F32
    )


def kernel(
    og_ref,
    in_ref,
    gp_ref,
    up_ref,
    gw_ref,
    uw_ref,
    dw_ref,
    gi_ref,
    ga_ref,
    ua_ref,
    dwv,
    gwv,
    uwv,
    gpv,
    upv,
    og,
    xg,
    xt,
    db,
    hb,
    hs,
    hr,
    ho,
    zs,
    zr,
    xs,
    xr,
    gacc,
    gs,
    gr,
    gz,
    gzr,
    load_sem,
    send_sem,
    r_og,
    r_in,
    r_rs,
    r_ag,
    r_gi,
):
    r = lax.axis_index("row")
    c = lax.axis_index("col")
    y, zh = r // 2, r % 2
    zl, x, k = c // 8, (c // 2) % 4, c % 2
    p = zl * NX + x
    pz = (1 - zl) * NX + x
    rz = y * 2 + 1 - zh

    def xmod(d):
        return (x + d) % NX

    def ymod(d):
        return (y + d) % NY

    dev_k = (r, c + 1 - 2 * k)
    dev_zl = (r, (1 - zl) * 8 + x * 2 + k)
    dev_zh = (rz, c)

    def dev_x(d):
        return (r, zl * 8 + xmod(d) * 2 + k)

    def dev_y(d, other=False):
        return (ymod(d) * 2 + (1 - zh if other else zh), c)

    dl = dw_ref.shape[1]

    barrier = pltpu.get_barrier_semaphore()
    peers = [dev_k, dev_zl, dev_zh]
    peers += [dev_x(d) for d in (1, 2, 3)]
    peers += [dev_y(d) for d in (1, 2, 3)]
    for dev in peers:
        pl.semaphore_signal(barrier, 1, device_id=dev, device_id_type=MESH)

    loads = {}

    def load(name, src, dst):
        cp = pltpu.make_async_copy(src, dst, load_sem.at[len(loads)])
        cp.start()
        loads[name] = cp

    load("og", og_ref, og.at[r])
    load("dw", dw_ref, dwv)
    load("in", in_ref, xg.at[r])
    load("gp", gp_ref, gpv)
    load("up", up_ref, upv)
    for u in AHEAD:
        j, c0, w = UNITS[u]
        for a, ref in ((0, gp_ref), (1, up_ref)):
            load((u, a), ref.at[j, :, pl.ds(c0, w)], db.at[a, p, k, j, :, pl.ds(c0, w)])
    load("gw", gw_ref, gwv)
    load("uw", uw_ref, uwv)
    loaded = set()

    def need(*names):
        for name in names:
            if name not in loaded:
                loaded.add(name)
                loads[name].wait()

    pl.semaphore_wait(barrier, len(peers))

    def send(src, dst, ssem, rsem, dev):
        pltpu.make_async_remote_copy(
            src_ref=src,
            dst_ref=dst,
            send_sem=send_sem.at[ssem],
            recv_sem=rsem,
            device_id=dev,
            device_id_type=MESH,
        ).start()

    def arrived(ref, sem):
        pltpu.make_async_copy(ref, ref, sem).wait()

    def o0(j):
        if j == 0:
            send(og_ref.at[:, j], og.at[r, :, j], 0, r_og.at[j, 0], dev_zh)
        for d in (2, 1, 3):
            send(og_ref.at[:, j], og.at[r, :, j], 0, r_og.at[j, 1], dev_y(d))
        if j == 0:
            for q in range(1, NJ):
                send(og_ref.at[:, q], og.at[r, :, q], 0, r_og.at[q, 0], dev_zh)
            send(in_ref, xg.at[r], 1, r_in.at[0], dev_zh)

    def o1(j):
        arrived(og.at[0, :, j], r_og.at[j, 0])
        ref = og.at[rz, :, j]
        for d in (2, 1, 3):
            send(ref, ref, 0, r_og.at[j, 1], dev_y(d))

    def i1(_):
        need("in")
        arrived(xg.at[0], r_in.at[0])
        ref = xg.at[pl.ds(y * 2, 2)]
        for d in (1, 3, 2):
            send(ref, ref, 1, r_in.at[1], dev_y(d))

    def i2(_):
        arrived(xg.at[pl.ds(0, 6)], r_in.at[1])
        per = NK * NJ * TB

        def turn(n, _):
            cols = pl.ds(pl.multiple_of(n * 128, 128), 128)
            xt[cols, :] = xg[:, :, :, :, cols].reshape(NP * per, 128).T
            return 0

        lax.fori_loop(0, dl // 128, turn, 0)

    def cols_of(u):
        _, c0, w = UNITS[u]
        return pl.ds(c0, w)

    seen_og = set()

    def s0(u):
        j, c0, w = UNITS[u]
        need("og", "dw")
        if j not in seen_og:
            seen_og.add(j)
            arrived(og.at[pl.ds(0, 6), :, j], r_og.at[j, 1])
        left = jnp.concatenate(
            [og[:, 1 - k, j].reshape(NP * TB, dl), og[:, k, j].reshape(NP * TB, dl)], axis=0
        )
        nt = 768 if w % 768 == 0 else 512

        def tile(n, _):
            rows = pl.ds(pl.multiple_of(c0 + n * nt, nt), nt)
            out = right_trans(left, dwv[rows, :])
            at = pl.ds(pl.multiple_of(n * nt, nt), nt)
            hs[u, :, :, at] = out[: NP * TB].astype(BF16).reshape(NP, TB, nt)
            ho[u, :, :, at] = out[NP * TB :].reshape(NP, TB, nt)
            return 0

        lax.fori_loop(0, w // nt, tile, 0)
        send(hs.at[u], hr.at[u], 3 + j, r_rs.at[u, 0], dev_k)

    def core_sum(u, q):
        return ho[u, q] + hr[u, q].astype(F32)

    def s1(u):
        j = UNITS[u][0]
        arrived(hr.at[u], r_rs.at[u, 0])
        if u in SUM_X_FIRST:
            for d in (1, 3, 2):
                for lane in range(NZL):
                    xs[u, d - 1, lane] = core_sum(u, lane * NX + xmod(d)).astype(BF16)
                send(xs.at[u, d - 1], xr.at[u, d - 1], 3 + j, r_rs.at[u, 1], dev_x(d))
        else:

            def add(i, _):
                zs[u, i] = core_sum(u, (1 - zl) * NX + i).astype(BF16)
                return 0

            lax.fori_loop(0, NX, add, 0)
            send(zs.at[u], zr.at[u], 3 + j, r_rs.at[u, 1], dev_zl)

    def s2(u):
        j = UNITS[u][0]
        if u in SUM_X_FIRST:
            arrived(xr.at[u], r_rs.at[u, 1])
            total = core_sum(u, pz)
            for d in (1, 2, 3):
                total = total + xr[u, d - 1, 1 - zl].astype(F32)
            zs[u, 0] = total.astype(BF16)
            send(zs.at[u, 0], zr.at[u, 0], 3 + j, r_rs.at[u, 2], dev_zl)
        else:
            arrived(zr.at[u], r_rs.at[u, 1])
            for d in (1, 3, 2):
                q = xmod(d)
                xs[u, d - 1, 0] = (core_sum(u, zl * NX + q) + zr[u, q].astype(F32)).astype(BF16)
                send(xs.at[u, d - 1, 0], xr.at[u, d - 1, 0], 3 + j, r_rs.at[u, 2], dev_x(d))

    class Gather:
        def __init__(self, u, kind):
            self.u, self.sem = u, kind * len(UNITS) + u
            if kind == 1:
                self.sem = len(UNITS) + AHEAD.index(u)
            self.send_sem = 3 + NJ + self.sem
            self.hidden = kind == 0 and u in AHEAD

        def piece(self, q):
            if self.hidden:
                return hb.at[AHEAD.index(self.u), q, k]
            return db.at[:, q, k, UNITS[self.u][0], :, cols_of(self.u)]

        def pieces(self, n):
            if self.hidden:
                return hb.at[AHEAD.index(self.u), pl.ds(0, n), 0]
            return db.at[:, pl.ds(0, n), 0, UNITS[self.u][0], :, cols_of(self.u)]

        def half(self, a, q):
            if self.hidden:
                h = WMAX // 2
                return hb.at[AHEAD.index(self.u), q, k, :, pl.ds(a * h, h)]
            return db.at[a, q, k, UNITS[self.u][0], :, cols_of(self.u)]

        def send(self, n, ref, dev):
            send(ref, ref, self.send_sem, r_ag.at[self.sem, n], dev)

        def arrived(self, n, count):
            arrived(self.pieces(count), r_ag.at[self.sem, n])

        def sent(self):
            if self.hidden:
                ref = db.at[0, pl.ds(0, 5), 0, :, :, cols_of(self.u)]
            else:
                ref = db.at[:, pl.ds(0, 5), 0, :, :, cols_of(self.u)]
            arrived(ref, send_sem.at[self.send_sem])

    def g3(g):
        ref = g.piece(p)
        g.send(1, ref, dev_x(1))
        g.send(1, ref, dev_x(3))
        g.send(0, ref, dev_zl)
        g.send(5, ref, dev_k)

    def g4(g, x_first):
        g.arrived(0, 1)
        ref = g.piece(pz)
        if not x_first:
            g.send(2, ref, dev_x(1))
            g.send(2, ref, dev_x(3))
        g.send(5, ref, dev_k)

    def sides(g, first, then, lane, relay, x_first):
        lo = lane * NX + xmod(3)
        hi = lane * NX + xmod(1)
        g.arrived(first, 2)
        if relay:
            g.send(then, g.half(0, lo), dev_x(1))
            g.send(then, g.half(1, hi), dev_x(3))
        if relay and x_first:
            g.send(2, g.piece(lo), dev_zl)
            g.send(2, g.piece(hi), dev_zl)
        g.send(5, g.piece(lo), dev_k)
        g.send(5, g.piece(hi), dev_k)

    def g5(g, x_first):
        sides(g, 1, 3, zl, True, x_first)

    def g6(g, x_first):
        sides(g, 2, 4, 1 - zl, not x_first, x_first)

    def g7(g, x_first):
        g.arrived(3, 1)
        ref = g.piece(zl * NX + xmod(2))
        if x_first:
            g.send(4, ref, dev_zl)
        g.send(5, ref, dev_k)

    def g8(g, x_first):
        g.arrived(4, 1)
        g.send(5, g.piece((1 - zl) * NX + xmod(2)), dev_k)

    main = {u: Gather(u, 0) for u in range(len(UNITS))}
    ahead = {u: Gather(u, 1) for u in AHEAD}

    def p3(u):
        need((u, 0), (u, 1))
        g3(ahead[u])

    def of_main(step):
        return lambda u: step(main[u], u in GATHER_X_FIRST)

    def of_ahead(step):
        return lambda u: step(ahead[u], False)

    def gradients(hidden, g, up):
        s = jax.nn.sigmoid(g)
        return hidden * up * s * (1.0 + g * (1.0 - s)), hidden * g * s

    def s3(u):
        need("gp", "up")
        j = UNITS[u][0]
        cols = cols_of(u)
        if u in SUM_X_FIRST:
            arrived(zr.at[u, 0], r_rs.at[u, 2])
            hidden = core_sum(u, p) + zr[u, 0].astype(F32)
            lane = zl
        else:
            arrived(xr.at[u, :, 0], r_rs.at[u, 2])
            hidden = core_sum(u, p) + zr[u, x].astype(F32)
            lane = 0
        for d in (1, 2, 3):
            hidden = hidden + xr[u, d - 1, lane].astype(F32)
        if u in AHEAD:
            hb[AHEAD.index(u), p, k] = hidden.astype(BF16)
        else:
            g = gpv[j, :, cols].astype(F32)
            up = upv[j, :, cols].astype(F32)
            dgate, dup = gradients(hidden, g, up)
            db[0, p, k, j, :, cols] = dgate.astype(BF16)
            db[1, p, k, j, :, cols] = dup.astype(BF16)
        g3(main[u])

    begun = set()

    def s9(u):
        j, c0, w = UNITS[u]
        cols = cols_of(u)
        need("gw", "uw")
        main[u].arrived(5, NP)
        if u in AHEAD:
            ahead[u].arrived(5, NP)
            ahead[u].sent()

            def make(n, _):
                q, kk = n // NK, n % NK
                g = db[0, q, kk, j, :, cols].astype(F32)
                up = db[1, q, kk, j, :, cols].astype(F32)
                dgate, dup = gradients(hb[AHEAD.index(u), q, kk].astype(F32), g, up)
                db[0, q, kk, j, :, cols] = dgate.astype(BF16)
                db[1, q, kk, j, :, cols] = dup.astype(BF16)
                return 0

            lax.fori_loop(0, NP * NK, make, 0)
        dgate = db[0, :, :, j, :, cols].reshape(NP * NK * TB, w)
        dup = db[1, :, :, j, :, cols].reshape(NP * NK * TB, w)
        out = right_trans(dgate, gwv[:, cols]) + right_trans(dup, uwv[:, cols])
        if j in begun:
            out = out + gacc[j]
        begun.add(j)
        gacc[j] = out

    def gs0(j):
        gs[j] = gacc[j].astype(BF16).reshape(NP, NK, TB, dl)
        for d in (1, 3, 2):
            q = ymod(d) * 2
            if j < NJ - 1:
                send(gs.at[j, pl.ds(q, 2)], gr.at[j, d - 1], 2, r_gi.at[j, 1], dev_y(d))
            else:
                send(gs.at[j, q + zh], gr.at[j, d - 1, 0], 2, r_gi.at[j, 1], dev_y(d))
                send(gs.at[j, q + 1 - zh], gr.at[j, d - 1, 1], 2, r_gi.at[j, 1], dev_y(d, True))
        if j == NJ - 1:
            send(gs.at[j, rz], gzr.at[j], 2, r_gi.at[j, 0], dev_zh)

    def rows_of(dest):
        return pl.ds(pl.multiple_of(dest * NK * TB, NK * TB), NK * TB)

    def g10(j):
        arrived(gr.at[j], r_gi.at[j, 1])

        def total(q):
            acc = gacc[j, rows_of(y * 2 + q), :].reshape(NK, TB, dl)
            for d in (1, 2, 3):
                acc = acc + gr[j, d - 1, q].astype(F32)
            return acc

        gz[j] = total(1 - zh).astype(BF16)
        send(gz.at[j], gzr.at[j], 2, r_gi.at[j, 0], dev_zh)
        gacc[j, rows_of(r), :] = total(zh).reshape(NK * TB, dl)

    def g11(j):
        arrived(gzr.at[j], r_gi.at[j, 0])
        acc = gacc[j, rows_of(r), :].reshape(NK, TB, dl) + gzr[j].astype(F32)
        if j == NJ - 1:
            arrived(gr.at[j], r_gi.at[j, 1])
            for d in (1, 2, 3):
                for e in (0, 1):
                    acc = acc + gr[j, d - 1, e].astype(F32)
        gi_ref[:, j] = acc.astype(BF16)

    def dw(n):
        c0, w = BLOCKS[n // 2]
        cols = pl.ds(c0, w)
        right = db[n % 2, :, :, :, :, cols].reshape(NP * NK * NJ * TB, w)
        out = jnp.dot(xt[...], right, preferred_element_type=F32)
        (ga_ref, ua_ref)[n % 2][:, cols] = out.astype(BF16)

    steps = dict(
        o0=o0, o1=o1, i1=i1, i2=i2, s0=s0, s1=s1, s2=s2, s3=s3, s9=s9, gs=gs0, g10=g10, g11=g11,
        dw=dw, p3=p3,
    )
    for n, step in enumerate((g4, g5, g6, g7, g8)):
        steps["s" + str(4 + n)] = of_main(step)
        steps["p" + str(4 + n)] = of_ahead(step)
    for name, arg in ORDER:
        steps[name](arg)
    for n in range(3):
        arrived(og.at[pl.ds(0, 7)], send_sem.at[n])
    for j in range(NJ):
        arrived(db.at[0, pl.ds(0, 5), 0], send_sem.at[3 + j])
    for g in main.values():
        g.sent()


def store(gi, ga, ua, gi_out, ga_out, ua_out, sem):
    half = ga.shape[0] // 2
    top, low = pl.ds(0, half), pl.ds(half, half)
    copies = [(gi, gi_out)]
    for src, dst in ((ga, ga_out), (ua, ua_out)):
        copies += [(src.at[top], dst.at[top]), (src.at[low], dst.at[low])]
    started = []
    for n, (src, dst) in enumerate(copies):
        cp = pltpu.make_async_copy(src, dst, sem.at[n])
        cp.start()
        started.append(cp)
    for cp in started:
        cp.wait()


def on_device(inputs, out_grad, gate_pre, up_pre, gate_weight, up_weight, down_weight):
    ff, dl = down_weight.shape
    nu = len(UNITS)
    tok = NP * NK * NJ * TB
    dma = pltpu.SemaphoreType.DMA
    vm = pltpu.VMEM
    hbm = pl.BlockSpec(memory_space=pl.ANY)
    whole = pl.BlockSpec(memory_space=pltpu.VMEM)
    grad_input, grad_gate, grad_up = pl.pallas_call(
        kernel,
        out_shape=(
            pltpu.VMEM((NK, NJ, TB, dl), BF16),
            pltpu.VMEM((dl, ff), BF16),
            pltpu.VMEM((dl, ff), BF16),
        ),
        in_specs=[hbm] * 7,
        out_specs=(whole, whole, whole),
        scratch_shapes=[
            vm((ff, dl), BF16),
            vm((dl, ff), BF16),
            vm((dl, ff), BF16),
            vm((NJ, TB, ff), BF16),
            vm((NJ, TB, ff), BF16),
            vm((NP, NK, NJ, TB, dl), BF16),
            vm((NP, NK, NJ, TB, dl), BF16),
            vm((dl, tok), BF16),
            vm((2, NP, NK, NJ, TB, ff), BF16),
            vm((max(1, len(AHEAD)), NP, NK, TB, WMAX), BF16),
            vm((nu, NP, TB, WMAX), BF16),
            vm((nu, NP, TB, WMAX), BF16),
            vm((nu, NP, TB, WMAX), F32),
            vm((nu, NX, TB, WMAX), BF16),
            vm((nu, NX, TB, WMAX), BF16),
            vm((nu, 3, NZL, TB, WMAX), BF16),
            vm((nu, 3, NZL, TB, WMAX), BF16),
            vm((NJ, NP * NK * TB, dl), F32),
            vm((NJ, NP, NK, TB, dl), BF16),
            vm((NJ, 3, 2, NK, TB, dl), BF16),
            vm((NJ, NK, TB, dl), BF16),
            vm((NJ, NK, TB, dl), BF16),
            dma((7 + 2 * len(AHEAD),)),
            dma((3 + NJ + nu + len(AHEAD),)),
            dma((NJ, 2)),
            dma((2,)),
            dma((nu, 3)),
            dma((nu + len(AHEAD), 6)),
            dma((NJ, 2)),
        ],
        compiler_params=pltpu.CompilerParams(
            collective_id=0, has_side_effects=True, vmem_limit_bytes=48 * 2**20
        ),
        cost_estimate=pl.CostEstimate(
            flops=10 * tok * dl * ff, bytes_accessed=10 * dl * ff, transcendentals=0
        ),
    )(
        out_grad.reshape(NK, NJ, TB, dl),
        inputs.reshape(NK, NJ, TB, dl),
        gate_pre.reshape(NJ, TB, ff),
        up_pre.reshape(NJ, TB, ff),
        gate_weight,
        up_weight,
        down_weight,
    )
    grad_input, grad_gate, grad_up = pl.pallas_call(
        store,
        out_shape=(
            jax.ShapeDtypeStruct((NK, NJ, TB, dl), BF16),
            jax.ShapeDtypeStruct((dl, ff), BF16),
            jax.ShapeDtypeStruct((dl, ff), BF16),
        ),
        in_specs=[whole] * 3,
        out_specs=(hbm, hbm, hbm),
        scratch_shapes=[dma((5,))],
        compiler_params=pltpu.CompilerParams(vmem_limit_bytes=4 * 2**20),
    )(*(pltpu.with_memory_space_constraint(a, pltpu.VMEM) for a in (grad_input, grad_gate, grad_up)))
    return (grad_input.reshape(NK * NJ * TB, dl), grad_gate, grad_up)


def solution(mesh):
    placed = (
        P("row", "col"),
        P("row", "col"),
        P("col", "row"),
        P("col", "row"),
        P("col", "row"),
        P("col", "row"),
        P("row", "col"),
    )
    return jax.shard_map(
        on_device,
        mesh=mesh,
        in_specs=placed,
        out_specs=(P("row", "col"), P("col", "row"), P("col", "row")),
        check_vma=False,
    )
```

```python
import jax
import jax.numpy as jnp
from jax import lax
from jax.experimental import pallas as pl
from jax.experimental.pallas import tpu as pltpu
from jax.sharding import PartitionSpec as P

BF16 = jnp.bfloat16
F32 = jnp.float32
MESH = pl.DeviceIdType.MESH
NY, NZH, NZL, NX, NK = 4, 2, 2, 4, 2
NP = NZL * NX
NJ = 3
TB = 16

UNITS = ((0, 0, 768), (0, 2304, 768), (0, 1536, 768), (0, 768, 768), (1, 768, 768), (2, 0, 768), (1, 0, 768), (1, 1536, 768), (1, 2304, 768), (2, 2304, 768), (2, 1536, 768), (2, 768, 768))
SUM_X_FIRST = (6, 0)
GATHER_X_FIRST = (8, 11, 0, 4, 10)
AHEAD = (0, 3, 2, 1)
BLOCKS = tuple(sorted({(c0, w) for _, c0, w in UNITS}))
WMAX = max(w for _, w in BLOCKS)

ORDER = (
    ("o0", 0), ("p3", 0), ("p3", 3), ("p3", 1), ("p3", 2), ("o1", 0), ("p5", 0), ("o0", 1),
    ("p5", 2), ("o1", 1), ("p5", 1), ("o0", 2), ("p5", 3), ("s0", 0), ("s0", 1), ("p4", 0),
    ("s0", 2), ("s1", 0), ("s1", 1), ("s0", 3), ("p4", 1), ("o1", 2), ("p4", 2), ("s1", 2),
    ("p7", 1), ("s0", 4), ("s1", 3), ("s0", 7), ("i1", 0), ("p6", 0), ("p4", 3), ("s0", 6),
    ("s2", 1), ("s1", 6), ("s1", 4), ("s2", 0), ("s0", 5), ("s0", 8), ("s2", 2), ("s1", 5),
    ("p6", 3), ("s2", 3), ("s0", 10), ("p7", 2), ("s3", 1), ("p6", 2), ("s1", 7), ("s0", 11),
    ("s3", 0), ("s2", 4), ("s2", 6), ("s3", 2), ("s2", 5), ("s0", 9), ("s1", 8), ("p6", 1),
    ("s3", 3), ("s1", 10), ("s4", 1), ("s2", 7), ("s5", 1), ("s3", 6), ("s5", 0), ("s4", 2),
    ("s1", 11), ("s1", 9), ("s3", 4), ("s6", 1), ("s4", 3), ("s2", 8), ("s5", 2), ("s3", 5),
    ("s7", 0), ("s5", 3), ("s7", 1), ("s3", 7), ("s5", 4), ("s6", 2), ("p8", 1), ("s8", 1),
    ("s2", 10), ("s9", 1), ("s3", 8), ("s7", 3), ("s6", 3), ("s7", 2), ("p7", 0), ("p7", 3),
    ("s4", 0), ("p8", 2), ("s5", 6), ("s2", 11), ("i2", 0), ("p8", 0), ("p8", 3), ("s6", 0),
    ("s2", 9), ("s4", 6), ("s4", 5), ("s7", 4), ("s8", 0), ("s5", 8), ("s8", 3), ("s5", 5),
    ("s8", 2), ("s9", 0), ("s4", 7), ("s3", 10), ("s9", 2), ("s6", 4), ("s6", 5), ("s6", 6),
    ("s3", 9), ("s4", 4), ("s7", 8), ("s8", 4), ("s3", 11), ("s9", 3), ("s7", 6), ("s6", 7),
    ("s7", 5), ("s9", 4), ("s8", 5), ("s5", 7), ("s8", 6), ("s5", 10), ("gs", 0), ("s4", 9),
    ("s4", 8), ("s9", 5), ("s6", 8), ("s8", 8), ("s5", 11), ("s5", 9), ("s9", 6), ("s8", 7),
    ("s9", 8), ("s7", 10), ("s7", 7), ("dw", 0), ("s7", 11), ("s6", 9), ("s4", 10), ("s9", 7),
    ("gs", 1), ("s6", 10), ("dw", 1), ("s8", 10), ("g10", 0), ("s4", 11), ("s7", 9), ("s6", 11),
    ("s8", 9), ("s8", 11), ("s9", 10), ("s9", 9), ("s9", 11), ("gs", 2), ("dw", 5), ("dw", 4),
    ("g11", 0), ("g10", 1), ("dw", 2), ("dw", 7), ("dw", 3), ("dw", 6), ("g11", 1), ("g11", 2),
)


def right_trans(left, right):
    return lax.dot_general(
        left, right, (((1,), (1,)), ((), ())), preferred_element_type=F32
    )


def kernel(
    og_ref,
    in_ref,
    gp_ref,
    up_ref,
    gw_ref,
    uw_ref,
    dw_ref,
    gi_ref,
    ga_ref,
    ua_ref,
    dwv,
    gwv,
    uwv,
    gpv,
    upv,
    og,
    xg,
    xt,
    db,
    hb,
    hs,
    hr,
    ho,
    zs,
    zr,
    xs,
    xr,
    gacc,
    gs,
    gr,
    gz,
    gzr,
    load_sem,
    send_sem,
    r_og,
    r_in,
    r_rs,
    r_ag,
    r_gi,
):
    r = lax.axis_index("row")
    c = lax.axis_index("col")
    y, zh = r // 2, r % 2
    zl, x, k = c // 8, (c // 2) % 4, c % 2
    p = zl * NX + x
    pz = (1 - zl) * NX + x
    rz = y * 2 + 1 - zh

    def xmod(d):
        return (x + d) % NX

    def ymod(d):
        return (y + d) % NY

    dev_k = (r, c + 1 - 2 * k)
    dev_zl = (r, (1 - zl) * 8 + x * 2 + k)
    dev_zh = (rz, c)

    def dev_x(d):
        return (r, zl * 8 + xmod(d) * 2 + k)

    def dev_y(d, other=False):
        return (ymod(d) * 2 + (1 - zh if other else zh), c)

    dl = dw_ref.shape[1]

    barrier = pltpu.get_barrier_semaphore()
    peers = [dev_k, dev_zl, dev_zh]
    peers += [dev_x(d) for d in (1, 2, 3)]
    peers += [dev_y(d) for d in (1, 2, 3)]
    for dev in peers:
        pl.semaphore_signal(barrier, 1, device_id=dev, device_id_type=MESH)

    loads = {}

    def load(name, src, dst):
        cp = pltpu.make_async_copy(src, dst, load_sem.at[len(loads)])
        cp.start()
        loads[name] = cp

    load("og", og_ref, og.at[r])
    load("dw", dw_ref, dwv)
    load("in", in_ref, xg.at[r])
    load("gp", gp_ref, gpv)
    load("up", up_ref, upv)
    for u in AHEAD:
        j, c0, w = UNITS[u]
        for a, ref in ((0, gp_ref), (1, up_ref)):
            load((u, a), ref.at[j, :, pl.ds(c0, w)], db.at[a, p, k, j, :, pl.ds(c0, w)])
    load("gw", gw_ref, gwv)
    load("uw", uw_ref, uwv)
    loaded = set()

    def need(*names):
        for name in names:
            if name not in loaded:
                loaded.add(name)
                loads[name].wait()

    pl.semaphore_wait(barrier, len(peers))

    def send(src, dst, ssem, rsem, dev):
        pltpu.make_async_remote_copy(
            src_ref=src,
            dst_ref=dst,
            send_sem=send_sem.at[ssem],
            recv_sem=rsem,
            device_id=dev,
            device_id_type=MESH,
        ).start()

    def arrived(ref, sem):
        pltpu.make_async_copy(ref, ref, sem).wait()

    def o0(j):
        if j == 0:
            send(og_ref.at[:, j], og.at[r, :, j], 0, r_og.at[j, 0], dev_zh)
        for d in (2, 1, 3):
            send(og_ref.at[:, j], og.at[r, :, j], 0, r_og.at[j, 1], dev_y(d))
        if j == 0:
            for q in range(1, NJ):
                send(og_ref.at[:, q], og.at[r, :, q], 0, r_og.at[q, 0], dev_zh)
            send(in_ref, xg.at[r], 1, r_in.at[0], dev_zh)

    def o1(j):
        arrived(og.at[0, :, j], r_og.at[j, 0])
        ref = og.at[rz, :, j]
        for d in (2, 1, 3):
            send(ref, ref, 0, r_og.at[j, 1], dev_y(d))

    def i1(_):
        need("in")
        arrived(xg.at[0], r_in.at[0])
        ref = xg.at[pl.ds(y * 2, 2)]
        for d in (1, 3, 2):
            send(ref, ref, 1, r_in.at[1], dev_y(d))

    def i2(_):
        arrived(xg.at[pl.ds(0, 6)], r_in.at[1])
        per = NK * NJ * TB

        def turn(n, _):
            cols = pl.ds(pl.multiple_of(n * 128, 128), 128)
            xt[cols, :] = xg[:, :, :, :, cols].reshape(NP * per, 128).T
            return 0

        lax.fori_loop(0, dl // 128, turn, 0)

    def cols_of(u):
        _, c0, w = UNITS[u]
        return pl.ds(c0, w)

    seen_og = set()

    def s0(u):
        j, c0, w = UNITS[u]
        need("og", "dw")
        if j not in seen_og:
            seen_og.add(j)
            arrived(og.at[pl.ds(0, 6), :, j], r_og.at[j, 1])
        left = jnp.concatenate(
            [og[:, 1 - k, j].reshape(NP * TB, dl), og[:, k, j].reshape(NP * TB, dl)], axis=0
        )
        nt = 768 if w % 768 == 0 else 512

        def tile(n, _):
            rows = pl.ds(pl.multiple_of(c0 + n * nt, nt), nt)
            out = right_trans(left, dwv[rows, :])
            at = pl.ds(pl.multiple_of(n * nt, nt), nt)
            hs[u, :, :, at] = out[: NP * TB].astype(BF16).reshape(NP, TB, nt)
            ho[u, :, :, at] = out[NP * TB :].reshape(NP, TB, nt)
            return 0

        lax.fori_loop(0, w // nt, tile, 0)
        send(hs.at[u], hr.at[u], 3 + j, r_rs.at[u, 0], dev_k)

    def core_sum(u, q):
        return ho[u, q] + hr[u, q].astype(F32)

    def s1(u):
        j = UNITS[u][0]
        arrived(hr.at[u], r_rs.at[u, 0])
        if u in SUM_X_FIRST:
            for d in (2, 1, 3):
                for lane in range(NZL):
                    xs[u, d - 1, lane] = core_sum(u, lane * NX + xmod(d)).astype(BF16)
                send(xs.at[u, d - 1], xr.at[u, d - 1], 3 + j, r_rs.at[u, 1], dev_x(d))
        else:

            def add(i, _):
                zs[u, i] = core_sum(u, (1 - zl) * NX + i).astype(BF16)
                return 0

            lax.fori_loop(0, NX, add, 0)
            send(zs.at[u], zr.at[u], 3 + j, r_rs.at[u, 1], dev_zl)

    def s2(u):
        j = UNITS[u][0]
        if u in SUM_X_FIRST:
            arrived(xr.at[u], r_rs.at[u, 1])
            total = core_sum(u, pz)
            for d in (1, 2, 3):
                total = total + xr[u, d - 1, 1 - zl].astype(F32)
            zs[u, 0] = total.astype(BF16)
            send(zs.at[u, 0], zr.at[u, 0], 3 + j, r_rs.at[u, 2], dev_zl)
        else:
            arrived(zr.at[u], r_rs.at[u, 1])
            for d in (2, 1, 3):
                q = xmod(d)
                xs[u, d - 1, 0] = (core_sum(u, zl * NX + q) + zr[u, q].astype(F32)).astype(BF16)
                send(xs.at[u, d - 1, 0], xr.at[u, d - 1, 0], 3 + j, r_rs.at[u, 2], dev_x(d))

    class Gather:
        def __init__(self, u, kind):
            self.u, self.sem = u, kind * len(UNITS) + u
            if kind == 1:
                self.sem = len(UNITS) + AHEAD.index(u)
            self.send_sem = 3 + NJ + self.sem
            self.hidden = kind == 0 and u in AHEAD

        def piece(self, q):
            if self.hidden:
                return hb.at[AHEAD.index(self.u), q, k]
            return db.at[:, q, k, UNITS[self.u][0], :, cols_of(self.u)]

        def pieces(self, n):
            if self.hidden:
                return hb.at[AHEAD.index(self.u), pl.ds(0, n), 0]
            return db.at[:, pl.ds(0, n), 0, UNITS[self.u][0], :, cols_of(self.u)]

        def half(self, a, q):
            if self.hidden:
                h = WMAX // 2
                return hb.at[AHEAD.index(self.u), q, k, :, pl.ds(a * h, h)]
            return db.at[a, q, k, UNITS[self.u][0], :, cols_of(self.u)]

        def send(self, n, ref, dev):
            send(ref, ref, self.send_sem, r_ag.at[self.sem, n], dev)

        def arrived(self, n, count):
            arrived(self.pieces(count), r_ag.at[self.sem, n])

        def sent(self):
            if self.hidden:
                ref = db.at[0, pl.ds(0, 5), 0, :, :, cols_of(self.u)]
            else:
                ref = db.at[:, pl.ds(0, 5), 0, :, :, cols_of(self.u)]
            arrived(ref, send_sem.at[self.send_sem])

    def g3(g):
        ref = g.piece(p)
        g.send(1, ref, dev_x(1))
        g.send(1, ref, dev_x(3))
        g.send(0, ref, dev_zl)
        g.send(5, ref, dev_k)

    def g4(g, x_first):
        g.arrived(0, 1)
        ref = g.piece(pz)
        if not x_first:
            g.send(2, ref, dev_x(1))
            g.send(2, ref, dev_x(3))
        g.send(5, ref, dev_k)

    def sides(g, first, then, lane, relay, x_first):
        lo = lane * NX + xmod(3)
        hi = lane * NX + xmod(1)
        g.arrived(first, 2)
        if relay:
            g.send(then, g.half(0, lo), dev_x(1))
            g.send(then, g.half(1, hi), dev_x(3))
        if relay and x_first:
            g.send(2, g.piece(lo), dev_zl)
            g.send(2, g.piece(hi), dev_zl)
        g.send(5, g.piece(lo), dev_k)
        g.send(5, g.piece(hi), dev_k)

    def g5(g, x_first):
        sides(g, 1, 3, zl, True, x_first)

    def g6(g, x_first):
        sides(g, 2, 4, 1 - zl, not x_first, x_first)

    def g7(g, x_first):
        g.arrived(3, 1)
        ref = g.piece(zl * NX + xmod(2))
        if x_first:
            g.send(4, ref, dev_zl)
        g.send(5, ref, dev_k)

    def g8(g, x_first):
        g.arrived(4, 1)
        g.send(5, g.piece((1 - zl) * NX + xmod(2)), dev_k)

    main = {u: Gather(u, 0) for u in range(len(UNITS))}
    ahead = {u: Gather(u, 1) for u in AHEAD}

    def p3(u):
        need((u, 0), (u, 1))
        g3(ahead[u])

    def of_main(step):
        return lambda u: step(main[u], u in GATHER_X_FIRST)

    def of_ahead(step):
        return lambda u: step(ahead[u], False)

    def gradients(hidden, g, up):
        s = jax.nn.sigmoid(g)
        return hidden * up * s * (1.0 + g * (1.0 - s)), hidden * g * s

    def s3(u):
        need("gp", "up")
        j = UNITS[u][0]
        cols = cols_of(u)
        if u in SUM_X_FIRST:
            arrived(zr.at[u, 0], r_rs.at[u, 2])
            hidden = core_sum(u, p) + zr[u, 0].astype(F32)
            lane = zl
        else:
            arrived(xr.at[u, :, 0], r_rs.at[u, 2])
            hidden = core_sum(u, p) + zr[u, x].astype(F32)
            lane = 0
        for d in (1, 2, 3):
            hidden = hidden + xr[u, d - 1, lane].astype(F32)
        if u in AHEAD:
            hb[AHEAD.index(u), p, k] = hidden.astype(BF16)
        else:
            g = gpv[j, :, cols].astype(F32)
            up = upv[j, :, cols].astype(F32)
            dgate, dup = gradients(hidden, g, up)
            db[0, p, k, j, :, cols] = dgate.astype(BF16)
            db[1, p, k, j, :, cols] = dup.astype(BF16)
        g3(main[u])

    begun = set()

    def s9(u):
        j, c0, w = UNITS[u]
        cols = cols_of(u)
        need("gw", "uw")
        main[u].arrived(5, NP)
        if u in AHEAD:
            ahead[u].arrived(5, NP)
            ahead[u].sent()

            def make(n, _):
                q, kk = n // NK, n % NK
                g = db[0, q, kk, j, :, cols].astype(F32)
                up = db[1, q, kk, j, :, cols].astype(F32)
                dgate, dup = gradients(hb[AHEAD.index(u), q, kk].astype(F32), g, up)
                db[0, q, kk, j, :, cols] = dgate.astype(BF16)
                db[1, q, kk, j, :, cols] = dup.astype(BF16)
                return 0

            lax.fori_loop(0, NP * NK, make, 0)
        dgate = db[0, :, :, j, :, cols].reshape(NP * NK * TB, w)
        dup = db[1, :, :, j, :, cols].reshape(NP * NK * TB, w)
        out = right_trans(dgate, gwv[:, cols]) + right_trans(dup, uwv[:, cols])
        if j in begun:
            out = out + gacc[j]
        begun.add(j)
        gacc[j] = out

    def gs0(j):
        gs[j] = gacc[j].astype(BF16).reshape(NP, NK, TB, dl)
        if j == NJ - 1:
            for other in (True, False):
                for d in (2, 1, 3):
                    q = ymod(d) * 2 + (1 - zh if other else zh)
                    slot = gr.at[j, d - 1, int(other)]
                    send(gs.at[j, q], slot, 2, r_gi.at[j, 1], dev_y(d, other))
                if other:
                    send(gs.at[j, rz], gzr.at[j], 2, r_gi.at[j, 0], dev_zh)
        else:
            for d in (2, 1, 3):
                rows = gs.at[j, pl.ds(ymod(d) * 2, 2)]
                send(rows, gr.at[j, d - 1], 2, r_gi.at[j, 1], dev_y(d))

    def rows_of(dest):
        return pl.ds(pl.multiple_of(dest * NK * TB, NK * TB), NK * TB)

    def g10(j):
        arrived(gr.at[j], r_gi.at[j, 1])

        def total(q):
            acc = gacc[j, rows_of(y * 2 + q), :].reshape(NK, TB, dl)
            for d in (1, 2, 3):
                acc = acc + gr[j, d - 1, q].astype(F32)
            return acc

        gz[j] = total(1 - zh).astype(BF16)
        send(gz.at[j], gzr.at[j], 2, r_gi.at[j, 0], dev_zh)
        gacc[j, rows_of(r), :] = total(zh).reshape(NK * TB, dl)

    def g11(j):
        arrived(gzr.at[j], r_gi.at[j, 0])
        acc = gacc[j, rows_of(r), :].reshape(NK, TB, dl) + gzr[j].astype(F32)
        if j == NJ - 1:
            arrived(gr.at[j], r_gi.at[j, 1])
            for d in (1, 2, 3):
                for e in (0, 1):
                    acc = acc + gr[j, d - 1, e].astype(F32)
        gi_ref[:, j] = acc.astype(BF16)

    def dw(n):
        c0, w = BLOCKS[n // 2]
        cols = pl.ds(c0, w)
        right = db[n % 2, :, :, :, :, cols].reshape(NP * NK * NJ * TB, w)
        out = jnp.dot(xt[...], right, preferred_element_type=F32)
        (ga_ref, ua_ref)[n % 2][:, cols] = out.astype(BF16)

    steps = dict(
        o0=o0, o1=o1, i1=i1, i2=i2, s0=s0, s1=s1, s2=s2, s3=s3, s9=s9, gs=gs0, g10=g10, g11=g11,
        dw=dw, p3=p3,
    )
    for n, step in enumerate((g4, g5, g6, g7, g8)):
        steps["s" + str(4 + n)] = of_main(step)
        steps["p" + str(4 + n)] = of_ahead(step)
    for name, arg in ORDER:
        steps[name](arg)
    for n in range(3):
        arrived(og.at[pl.ds(0, 7)], send_sem.at[n])
    for j in range(NJ):
        arrived(db.at[0, pl.ds(0, 5), 0], send_sem.at[3 + j])
    for g in main.values():
        g.sent()


def store(gi, ga, ua, gi_out, ga_out, ua_out, sem):
    half = ga.shape[0] // 2
    top, low = pl.ds(0, half), pl.ds(half, half)
    copies = [(gi, gi_out)]
    for src, dst in ((ga, ga_out), (ua, ua_out)):
        copies += [(src.at[top], dst.at[top]), (src.at[low], dst.at[low])]
    started = []
    for n, (src, dst) in enumerate(copies):
        cp = pltpu.make_async_copy(src, dst, sem.at[n])
        cp.start()
        started.append(cp)
    for cp in started:
        cp.wait()


def on_device(inputs, out_grad, gate_pre, up_pre, gate_weight, up_weight, down_weight):
    ff, dl = down_weight.shape
    nu = len(UNITS)
    tok = NP * NK * NJ * TB
    dma = pltpu.SemaphoreType.DMA
    vm = pltpu.VMEM
    hbm = pl.BlockSpec(memory_space=pl.ANY)
    whole = pl.BlockSpec(memory_space=pltpu.VMEM)
    grad_input, grad_gate, grad_up = pl.pallas_call(
        kernel,
        out_shape=(
            pltpu.VMEM((NK, NJ, TB, dl), BF16),
            pltpu.VMEM((dl, ff), BF16),
            pltpu.VMEM((dl, ff), BF16),
        ),
        in_specs=[hbm] * 7,
        out_specs=(whole, whole, whole),
        scratch_shapes=[
            vm((ff, dl), BF16),
            vm((dl, ff), BF16),
            vm((dl, ff), BF16),
            vm((NJ, TB, ff), BF16),
            vm((NJ, TB, ff), BF16),
            vm((NP, NK, NJ, TB, dl), BF16),
            vm((NP, NK, NJ, TB, dl), BF16),
            vm((dl, tok), BF16),
            vm((2, NP, NK, NJ, TB, ff), BF16),
            vm((max(1, len(AHEAD)), NP, NK, TB, WMAX), BF16),
            vm((nu, NP, TB, WMAX), BF16),
            vm((nu, NP, TB, WMAX), BF16),
            vm((nu, NP, TB, WMAX), F32),
            vm((nu, NX, TB, WMAX), BF16),
            vm((nu, NX, TB, WMAX), BF16),
            vm((nu, 3, NZL, TB, WMAX), BF16),
            vm((nu, 3, NZL, TB, WMAX), BF16),
            vm((NJ, NP * NK * TB, dl), F32),
            vm((NJ, NP, NK, TB, dl), BF16),
            vm((NJ, 3, 2, NK, TB, dl), BF16),
            vm((NJ, NK, TB, dl), BF16),
            vm((NJ, NK, TB, dl), BF16),
            dma((7 + 2 * len(AHEAD),)),
            dma((3 + NJ + nu + len(AHEAD),)),
            dma((NJ, 2)),
            dma((2,)),
            dma((nu, 3)),
            dma((nu + len(AHEAD), 6)),
            dma((NJ, 2)),
        ],
        compiler_params=pltpu.CompilerParams(
            collective_id=0, has_side_effects=True, vmem_limit_bytes=48 * 2**20
        ),
        cost_estimate=pl.CostEstimate(
            flops=10 * tok * dl * ff, bytes_accessed=10 * dl * ff, transcendentals=0
        ),
    )(
        out_grad.reshape(NK, NJ, TB, dl),
        inputs.reshape(NK, NJ, TB, dl),
        gate_pre.reshape(NJ, TB, ff),
        up_pre.reshape(NJ, TB, ff),
        gate_weight,
        up_weight,
        down_weight,
    )
    grad_input, grad_gate, grad_up = pl.pallas_call(
        store,
        out_shape=(
            jax.ShapeDtypeStruct((NK, NJ, TB, dl), BF16),
            jax.ShapeDtypeStruct((dl, ff), BF16),
            jax.ShapeDtypeStruct((dl, ff), BF16),
        ),
        in_specs=[whole] * 3,
        out_specs=(hbm, hbm, hbm),
        scratch_shapes=[dma((5,))],
        compiler_params=pltpu.CompilerParams(vmem_limit_bytes=4 * 2**20),
    )(*(pltpu.with_memory_space_constraint(a, pltpu.VMEM) for a in (grad_input, grad_gate, grad_up)))
    return (grad_input.reshape(NK * NJ * TB, dl), grad_gate, grad_up)


def solution(mesh):
    placed = (
        P("row", "col"),
        P("row", "col"),
        P("col", "row"),
        P("col", "row"),
        P("col", "row"),
        P("col", "row"),
        P("row", "col"),
    )
    return jax.shard_map(
        on_device,
        mesh=mesh,
        in_specs=placed,
        out_specs=(P("row", "col"), P("col", "row"), P("col", "row")),
        check_vma=False,
    )
```
